256 devices in a mesh: dp: 32 (over z, y_hi, core), tensor: 8 (over y_lo, x).
Axes of the slice: x: 4, y: 4 (y_hi: 2, y_lo: 2; y = y_hi * 2 + y_lo), z: 8, core: 2. Of those that a mesh axis runs over, the one named last changes fastest.
Arguments:
- hidden: bfloat16 [16384, 8192], P(('dp', 'tensor')), may hold values from -6 to 6
- gain: float32 [8192], replicated, may hold values from 0.1 to 1.9
- segment_ids: int32 [32, 512], P('dp'), may hold values from 0 to 7, never falling along the last dimension, each value on 1 to 256 neighbouring positions
- w_query: bfloat16 [8192, 4096], P('dp', 'tensor'), may hold values from -1.5 to 1.5
- key_matrix: bfloat16 [8192, 1024], P('dp', 'tensor'), may hold values from -0.0625 to 0.0625
- value_matrix: bfloat16 [8192, 1024], P('dp', 'tensor'), may hold values from -0.0625 to 0.0625
- w_out: bfloat16 [4096, 8192], P('tensor', 'dp'), may hold values from -0.09375 to 0.09375
Outputs:
- attended: bfloat16 [16384, 8192], P(('dp', 'tensor'))
The draws below stay inside these ranges and needn't reach their ends.
All inputs are finite; a program needn't handle non-finite values.
Results may differ from the reference program's by a relative error of at most 0.018.
Values may be sent and summed in bfloat16 or wider, within the bound.
A program may use at most 128 MiB of HBM per device.

```python
import math
import jax
import jax.numpy as jnp
import numpy as np
from jax import lax

MODEL_WIDTH = 8192
KEY_VALUE_HEADS = 8
HEAD_SIZE = 128
QUERY_HEAD_COUNT = 32
ROW_TOKEN_COUNT = 512
TOKENS = 16384
N_DP = 32
N_TENSOR = 8


def key_base(key):
    return jax.random.normal(jax.random.fold_in(key, 17), (MODEL_WIDTH, KEY_VALUE_HEADS * HEAD_SIZE), jnp.float32) * MODEL_WIDTH ** (-0.5)


def draw_hidden(key, part):
    key = jax.random.fold_in(key, 1)
    base = jax.random.normal(key, (TOKENS, MODEL_WIDTH), jnp.float32)
    values = base
    return jnp.clip(values, -6.0, 6.0).astype(jnp.bfloat16)


def draw_key_matrix(key, part):
    common_heads = key_base(key)
    return jnp.clip(common_heads, -0.0625, 0.0625).astype(jnp.bfloat16)


def draw_w_query(key, part):
    key = jax.random.fold_in(key, 5)
    noise = jax.random.normal(key, (MODEL_WIDTH, QUERY_HEAD_COUNT * HEAD_SIZE), jnp.float32) * MODEL_WIDTH ** (-0.5)
    values = noise
    return jnp.clip(values, -1.5, 1.5).astype(jnp.bfloat16)


def levels(rng, dims, pieces, low, high):
    factor_of = 1.0
    for position, parts in pieces:
        heights = jax.random.uniform(jax.random.fold_in(jax.random.fold_in(rng, 6), position), (parts,), jnp.float32, low / len(pieces), high / len(pieces))
        factor_of = factor_of * jnp.repeat(jnp.exp(heights), dims[position] // parts).reshape((-1,) + (1,) * (len(dims) - 1 - position))
    return factor_of


def split_up(count, total, limit, lean):
    loads = [(1 << 20) // math.isqrt(grade ** lean) + 1 for grade in range(2, count + 1)]
    spare, holding = total - limit - (count - 1), [1] * (count - 1)
    while spare > 0:
        candidates = [i for i in range(count - 1) if holding[i] < limit]
        whole, budget = sum([loads[i] for i in candidates]), spare
        for i in candidates:
            more = min(limit - holding[i], max(1, budget * loads[i] // whole), spare)
            holding[i] = holding[i] + more
            spare = spare - more
    return np.array([limit] + holding)


def uneven(key, amount, total, bound, skew):
    if amount == 2:
        one = jax.random.randint(key, (), max(1, total - bound), min(bound, total - 1) + 1)
        return jnp.stack([one, total - one])
    sizes = jnp.asarray(split_up(amount, total, bound, skew), jnp.int32)
    couples = (amount - 1) // 2
    source_of, taker = sizes[1:1 + 2 * couples:2], sizes[2:2 + 2 * couples:2]
    room = jnp.minimum(source_of - 1, bound - taker)
    passed = jax.random.randint(jax.random.fold_in(key, 1), (couples,), 0, 1 << 20) % (room + 1)
    sizes = sizes.at[1:1 + 2 * couples:2].set(source_of - passed).at[2:2 + 2 * couples:2].set(taker + passed)
    return sizes[jax.random.permutation(jax.random.fold_in(key, 2), amount)]


def scatter_about(stream_key, shape, spread, reach, shards=(), kind=jnp.bfloat16):
    drawn = spread * jax.random.normal(stream_key, shape, jnp.float32)
    if shards:
        drawn = drawn * levels(stream_key, shape, shards, -0.22, 0.18)
    return jnp.clip(drawn, -reach, reach).astype(kind)


def setup_inputs(seed: int = 0) -> dict:
    key_of = jax.random.split(jax.random.key(seed), 8)
    return {
        "hidden": draw_hidden(jax.random.fold_in(key_of[7], 71), 0),
        "gain": jnp.clip(1.0 + 0.18 * jax.random.normal(key_of[1], (MODEL_WIDTH,), jnp.float32), 0.1, 1.9),
        "segment_ids": jax.vmap(lambda own: jnp.searchsorted(jnp.cumsum(uneven(own, 8, ROW_TOKEN_COUNT, ROW_TOKEN_COUNT // 2, 2)), jnp.arange(ROW_TOKEN_COUNT), side="right"))(jax.random.split(key_of[2], N_DP)).reshape((N_DP, ROW_TOKEN_COUNT)).astype(jnp.int32),
        "w_query": draw_w_query(jax.random.fold_in(key_of[7], 71), 0),
        "key_matrix": draw_key_matrix(jax.random.fold_in(key_of[7], 71), 0),
        "value_matrix": scatter_about(key_of[5], (MODEL_WIDTH, KEY_VALUE_HEADS * HEAD_SIZE), MODEL_WIDTH ** -0.5, 0.0625, ((0, 32), (1, 8))),
        "w_out": scatter_about(key_of[6], (QUERY_HEAD_COUNT * HEAD_SIZE, MODEL_WIDTH), (QUERY_HEAD_COUNT * HEAD_SIZE) ** -0.5, 0.09375, ((0, 8), (1, 32))),
    }


def rms_norm(values, gain):
    expanded_heads = values.astype(jnp.float32)
    inv_rms = lax.rsqrt(lax.optimization_barrier(jnp.mean(expanded_heads * expanded_heads, axis=-1, keepdims=True)) + 1e-05)
    return (expanded_heads * inv_rms * gain).astype(jnp.bfloat16)

def seg_positions(segments):
    length = segments.shape[0]
    earlier = lax.optimization_barrier(jnp.sum((segments[None, :] < segments[:, None]).astype(jnp.int32), axis=1))
    return (jnp.arange(length, dtype=jnp.int32) - earlier).astype(jnp.float32)

def apply_rotary(heads, token_places):
    half_width = heads.shape[-1] // 2
    freq_index = jnp.arange(half_width, dtype=jnp.float32)
    inverse = jnp.exp(freq_index * (-2.0 * math.log(500000.0) / heads.shape[-1]))
    angles = token_places[:, None] * inverse[None, :]
    cosine = jnp.cos(angles)[:, None, :]
    sine_part = jnp.sin(angles)[:, None, :]
    first_half = heads[..., :half_width]
    second = heads[..., half_width:]
    return jnp.concatenate([first_half * cosine - second * sine_part, second * cosine + first_half * sine_part], axis=-1)

def attend(query_heads, key_head_rows, value_head_rows, segments):
    length, kv_heads, head_width = key_head_rows.shape
    grouped = query_heads.reshape(length, kv_heads, -1, head_width)
    scores = jnp.einsum('qkgd,skd->kgqs', grouped.astype(jnp.float32), key_head_rows.astype(jnp.float32)) / math.sqrt(head_width)
    position_ids = jnp.arange(length, dtype=jnp.int32)
    allowed = (segments[:, None] == segments[None, :]) & (position_ids[None, :] <= position_ids[:, None])
    scores = jnp.where(allowed, scores, jnp.float32(-1e+30))
    row_max = lax.optimization_barrier(jnp.max(scores, axis=-1, keepdims=True))
    exponent = jnp.exp(scores - row_max)
    weights = (exponent / lax.optimization_barrier(jnp.sum(exponent, axis=-1, keepdims=True))).astype(jnp.bfloat16)
    mixed_heads = jnp.einsum('kgqs,skd->qkgd', weights.astype(jnp.float32), value_head_rows.astype(jnp.float32))
    return mixed_heads.reshape(length, -1).astype(jnp.bfloat16)

def reference(hidden, gain, segment_ids, w_query, key_matrix, value_matrix, w_out):

    def one_group(operands):
        rows_in, segments = operands
        scaled_input = rms_norm(rows_in, gain)
        token_places = seg_positions(segments)
        query_heads = apply_rotary(jnp.dot(scaled_input, w_query, preferred_element_type=jnp.float32).reshape(ROW_TOKEN_COUNT, QUERY_HEAD_COUNT, HEAD_SIZE), token_places).astype(jnp.bfloat16)
        key_head_rows = apply_rotary(jnp.dot(scaled_input, key_matrix, preferred_element_type=jnp.float32).reshape(ROW_TOKEN_COUNT, KEY_VALUE_HEADS, HEAD_SIZE), token_places).astype(jnp.bfloat16)
        value_head_rows = jnp.dot(scaled_input, value_matrix, preferred_element_type=jnp.float32).astype(jnp.bfloat16).reshape(ROW_TOKEN_COUNT, KEY_VALUE_HEADS, HEAD_SIZE)
        mixed_heads = attend(query_heads, key_head_rows, value_head_rows, segments)
        block_width = QUERY_HEAD_COUNT * HEAD_SIZE // N_TENSOR
        summed = jnp.zeros((ROW_TOKEN_COUNT, MODEL_WIDTH), jnp.float32)
        for block_index in range(N_TENSOR):
            low = block_index * block_width
            partial_value = jnp.dot(mixed_heads[:, low:low + block_width], w_out[low:low + block_width], preferred_element_type=jnp.float32)
            rounded = lax.optimization_barrier(partial_value.astype(jnp.bfloat16))
            summed = summed + rounded.astype(jnp.float32)
        return summed.astype(jnp.bfloat16)
    grouped = lax.map(one_group, (hidden.reshape(N_DP, ROW_TOKEN_COUNT, MODEL_WIDTH), segment_ids))
    return grouped.reshape(TOKENS, MODEL_WIDTH)
```

```python
import functools
import math

import jax
import jax.numpy as jnp
from jax import lax
from jax.experimental import pallas as pl
from jax.experimental.pallas import tpu as pltpu
from jax.sharding import PartitionSpec as P

MESH = pl.DeviceIdType.MESH
BF = jnp.bfloat16
F32 = jnp.float32
HEAD = 128
VMEM_LIMIT = 56 * 2**20

RELS = ((0, 0), (1, 1), (1, 0), (0, 1))
SLOT = {r: i for i, r in enumerate(RELS)}


def place():
    dp = lax.axis_index("dp")
    t = lax.axis_index("tensor")
    return t % 4, (dp // 2) % 2, t // 4, dp // 4, dp % 2


def device(x, yh, yl, z, k):
    return (z * 4 + yh * 2 + k, yl * 4 + x)


def flip(v, f):
    return 1 - v if f else v


class Copies:
    def __init__(self, send, recv):
        self.send, self.recv, self.n, self.open = send, recv, 0, []

    def to(self, src, dst, dev):
        i = self.n
        self.n += 1
        return pltpu.make_async_remote_copy(
            src_ref=src, dst_ref=dst, send_sem=self.send.at[i], recv_sem=self.recv.at[i],
            device_id=dev, device_id_type=MESH)

    def go(self, src, dst, dev):
        cp = self.to(src, dst, dev)
        cp.start()
        self.open.append(cp)
        return cp

    def finish(self):
        for cp in self.open:
            cp.wait_send()


N_A = 80


def project_kernel(hid, gain, wq, wk, wv, wo, tab,
                   qkv, tab_out, wo_all,
                   xn, xs, wa, wb, part, got, tab_in, send, recv, swap_send, swap_recv, got_sem):
    x, yh, yl, z, k = place()
    sib = device(x, yh, yl, z, 1 - k)
    swapped = device(x, yh, k, z, yl)
    cps = Copies(send, recv)

    def ydev(r):
        return device(x, flip(yh, r[0]), flip(yl, r[1]), z, k)

    def xdev(d):
        return device((x + d + 4) % 4, yh, yl, z, k)

    def zdev(d):
        return device(x, yh, yl, (z + d + 8) % 8, k)

    bar = pltpu.get_barrier_semaphore()
    for dev in [ydev(r) for r in RELS[1:]] + [xdev(d) for d in (1, 2, 3)] + [zdev(1), zdev(-1), sib]:
        pl.semaphore_signal(bar, inc=1, device_id=dev, device_id_type=MESH)

    @pl.when(k != yl)
    def _():
        pl.semaphore_signal(bar, inc=1, device_id=swapped, device_id_type=MESH)

    pl.semaphore_wait(bar, 9 + (k + yl) % 2)

    rows = pl.ds(pl.multiple_of(z * 256, 256), 256)
    mine = [
        (wq, wa.at[rows, :]),
        (wk, wb.at[rows, pl.ds(0, 128)]),
        (wv, wb.at[rows, pl.ds(128, 128)]),
        (wo, wo_all.at[z, pl.ds(pl.multiple_of(k * 512, 512), 512), :]),
    ]
    theirs = [
        (wq, wa.at[rows, :]),
        (wk, wb.at[rows, pl.ds(0, 128)]),
        (wv, wb.at[rows, pl.ds(128, 128)]),
        (wo, wo_all.at[z, pl.ds(pl.multiple_of(yl * 512, 512), 512), :]),
    ]

    @pl.when(k != yl)
    def _():
        for i, (s, d) in enumerate(theirs):
            pltpu.make_async_remote_copy(
                src_ref=s, dst_ref=d, send_sem=swap_send.at[i], recv_sem=swap_recv.at[i],
                device_id=swapped, device_id_type=MESH).start()

    @pl.when(k == yl)
    def _():
        for i, (s, d) in enumerate(mine):
            pltpu.make_async_copy(s, d, swap_recv.at[i]).start()

    def wait_swap(i):
        s, d = mine[i]
        pltpu.make_async_copy(s, d, swap_recv.at[i]).wait()

    h = hid[...].astype(F32)
    inv = lax.rsqrt(jnp.mean(h * h, axis=-1, keepdims=True) + 1e-5)

    def slice_norm(r, store):
        yy = flip(yh, r[0]) * 2 + flip(yl, r[1])
        for zz in range(8):
            cols = pl.ds(pl.multiple_of((zz * 4 + yy) * 256, 256), 256)
            v = hid[:, cols].astype(F32) * inv * gain[:, cols]
            store(zz, v.astype(BF))

    for r in (1, 2, 3):
        def put(zz, v, r=r):
            xn[r - 1, :, zz * 256:(zz + 1) * 256] = v
        slice_norm(RELS[r], put)

    ysend = {}
    for r in (1, 2, 3):
        ysend[r] = cps.go(xn.at[r - 1], xs.at[r, k, x], ydev(RELS[r]))

    def put0(zz, v):
        xs[0, k, x, :, zz * 256:(zz + 1) * 256] = v
    slice_norm(RELS[0], put0)

    xgot = {}
    sibs = {}

    def spread(r):
        for d in (2, 1, 3):
            xgot[r, d] = cps.go(xs.at[r, k, x], xs.at[r, k, x], xdev(d))
        sibs[r, 0] = cps.go(xs.at[r, k, x], xs.at[r, k, x], sib)

    def spread_sib(r):
        for d in (1, 3, 2):
            xgot[r, d].wait_recv()
            src = xs.at[r, k, (x - d + 4) % 4]
            sibs[r, d] = cps.go(src, src, sib)

    def wait_sib(r):
        for d in (0, 1, 3, 2):
            sibs[r, d].wait_recv()

    spread(0)

    tab_cp = cps.go(tab, tab_in, sib)

    ring = {}

    def ring_step(name, at, s):
        for hf in (0, 1):
            for d in (1, -1):
                if s == 3 and hf != (0 if d == 1 else 1):
                    continue
                if s > 0:
                    ring[name, s - 1, hf, d].wait_recv()
                b = at((z - d * s + 8) % 8, hf)
                ring[name, s, hf, d] = cps.go(b, b, zdev(d))

    def ring_end(name):
        ring[name, 2, 1, 1].wait_recv()
        ring[name, 2, 0, -1].wait_recv()
        ring[name, 3, 0, 1].wait_recv()
        ring[name, 3, 1, -1].wait_recv()

    def at_a(b, hf):
        return wa.at[pl.ds(pl.multiple_of(b * 256 + hf * 128, 128), 128), :]

    def at_b(b, hf):
        return wb.at[pl.ds(pl.multiple_of(b * 256 + hf * 128, 128), 128), :]

    def at_o(b, hf):
        return wo_all.at[b, pl.ds(pl.multiple_of(k * 512 + hf * 256, 256), 256), :]

    def compute(r, w_ref, c0, width):
        def one(c, carry):
            lhs = xs[r, c].reshape(256, 2048)
            part[r, c, :, c0:c0 + width] = jnp.dot(
                lhs, w_ref[...], preferred_element_type=F32).astype(BF)
            return carry
        lax.fori_loop(0, 2, one, 0)
        a, b = RELS[r]
        for e in (1, 0):
            if (a, e) == (0, 0):
                continue
            c = flip(yl, e)
            dst_rows = pl.ds(pl.multiple_of(flip(yl, b) * 256, 256), 256)
            slot = SLOT[(a, e)] - 1
            i = cps.n
            cps.n += 1
            cp = pltpu.make_async_remote_copy(
                src_ref=part.at[r, c, :, pl.ds(c0, width)],
                dst_ref=got.at[slot, dst_rows, pl.ds(c0, width)],
                send_sem=send.at[i], recv_sem=got_sem.at[slot],
                device_id=ydev((a, e)), device_id_type=MESH)
            cp.start()
            cps.open.append(cp)

    def comp_a(r):
        compute(r, wa, 0, 512)

    def comp_b(r):
        compute(r, wb, 512, 256)

    wait_swap(0)
    ring_step("a", at_a, 0)
    ring_step("a", at_a, 1)
    ysend[1].wait_recv()
    spread(1)
    ring_step("a", at_a, 2)
    wait_swap(1)
    wait_swap(2)
    ring_step("b", at_b, 0)
    ysend[2].wait_recv()
    spread(2)
    ysend[3].wait_recv()
    spread(3)
    ring_step("a", at_a, 3)
    ring_step("b", at_b, 1)
    spread_sib(0)
    ring_end("a")
    ring_step("b", at_b, 2)
    wait_sib(0)
    comp_a(0)
    wait_swap(3)
    ring_step("b", at_b, 3)
    ring_step("o", at_o, 0)
    spread_sib(1)
    wait_sib(1)
    comp_a(1)
    ring_end("b")
    comp_b(0)
    comp_b(1)
    ring_step("o", at_o, 1)
    spread_sib(2)
    wait_sib(2)
    comp_a(2)
    comp_b(2)
    ring_step("o", at_o, 2)
    spread_sib(3)
    wait_sib(3)
    comp_a(3)
    comp_b(3)
    ring_step("o", at_o, 3)

    tab_cp.wait_recv()
    keep = k == yl
    tab_out[...] = jnp.where(keep, tab[...], tab_in[...])
    ring_end("o")
    half = wo_all.at[:, pl.ds(pl.multiple_of(k * 512, 512), 512), :]
    wo_cp = cps.go(half, half, sib)

    for slot in range(3):
        pltpu.make_async_copy(got.at[slot], got.at[slot], got_sem.at[slot]).wait()
    for b in (0, 1):
        r = SLOT[(0, b)]
        rows_b = pl.ds(pl.multiple_of(flip(yl, b) * 256, 256), 256)
        total = part[r, yl].astype(F32)
        for slot in range(3):
            total += got[slot, rows_b, :].astype(F32)
        qkv[rows_b, :] = total
    wo_cp.wait_recv()

    @pl.when(k != yl)
    def _():
        for i, (s, d) in enumerate(theirs):
            pltpu.make_async_remote_copy(
                src_ref=s, dst_ref=d, send_sem=swap_send.at[i], recv_sem=swap_recv.at[i],
                device_id=swapped, device_id_type=MESH).wait_send()
    cps.finish()


def attend_kernel(qkv, tab, mixed):
    cos = tab[:, 0:128]
    sin = tab[:, 128:256]

    def rotate(u):
        return (u * cos + pltpu.roll(u, 64, axis=1) * sin).astype(BF)

    keys = rotate(qkv[:, 512:640])
    values = qkv[:, 640:768].astype(BF)
    queries = [rotate(qkv[:, i * 128:(i + 1) * 128]) for i in range(4)]
    scale = 1.0 / math.sqrt(HEAD)
    for i in range(4):
        lo, hi = i * 128, (i + 1) * 128
        q = jnp.concatenate([queries[j][lo:hi] for j in range(4)], axis=0)
        s = lax.dot_general(q, keys[:hi], (((1,), (1,)), ((), ())), preferred_element_type=F32) * scale
        where_i = lax.broadcasted_iota(jnp.int32, (128, hi), 0) + lo
        where_s = lax.broadcasted_iota(jnp.int32, (128, hi), 1)
        start = where_i - tab[lo:hi, 256:257].astype(jnp.int32)
        ok = (where_s <= where_i) & (where_s >= start)
        s = jnp.where(ok[None], s.reshape(4, 128, hi), -1e30)
        e = jnp.exp(s - jnp.max(s, axis=-1, keepdims=True))
        w = (e / jnp.sum(e, axis=-1, keepdims=True)).astype(BF)
        o = jnp.dot(w.reshape(512, hi), values[:hi], preferred_element_type=F32).astype(BF)
        for j in range(4):
            mixed[lo:hi, j * 128:(j + 1) * 128] = o[j * 128:(j + 1) * 128]


N_C = 40


def output_kernel(mixed, wo_all, out,
                  m, wo, part, rx, slab, ry, send, recv, m_send, m_recv, wo_sem):
    x, yh, yl, z, k = place()
    cps = Copies(send, recv)
    sib = device(x, yh, yl, z, 1 - k)

    def ydev(r):
        return device(x, flip(yh, r[0]), flip(yl, r[1]), z, k)

    def xdev(d):
        return device((x + d + 4) % 4, yh, yl, z, k)

    def mdev(r):
        return device(x, flip(yh, r[0]), flip(yl, r[1]), z, yl)

    wo_cp = pltpu.make_async_copy(wo_all, wo, wo_sem)
    wo_cp.start()

    bar = pltpu.get_barrier_semaphore()
    for dev in [ydev(r) for r in RELS[1:]] + [xdev(d) for d in (1, 2, 3)]:
        pl.semaphore_signal(bar, inc=1, device_id=dev, device_id_type=MESH)

    for a in (0, 1):
        for j in (0, 1):
            src = device(x, flip(yh, a), k, z, j)
            if a == 0:
                @pl.when((k != yl) | (k != j))
                def _():
                    pl.semaphore_signal(bar, inc=1, device_id=src, device_id_type=MESH)
            else:
                pl.semaphore_signal(bar, inc=1, device_id=src, device_id_type=MESH)
    pl.semaphore_wait(bar, 9 + (k + yl) % 2)

    order = (2, 1, 3, 0)
    sends = []
    for n, d in enumerate(order):
        xx = (x + d) % 4
        src = mixed.at[:, xx]
        dst = m.at[yh, :, xx, :, pl.ds(pl.multiple_of(k * 512, 512), 512)]
        for r in (2, 1, 3):
            cp = pltpu.make_async_remote_copy(
                src_ref=src, dst_ref=dst, send_sem=m_send.at[n, r], recv_sem=m_recv.at[n, yh, k],
                device_id=mdev(RELS[r]), device_id_type=MESH)
            cp.start()
            sends.append(cp)

        @pl.when(k == yl)
        def _():
            pltpu.make_async_copy(src, dst, m_recv.at[n, yh, k]).start()

        @pl.when(k != yl)
        def _():
            pltpu.make_async_remote_copy(
                src_ref=src, dst_ref=dst, send_sem=m_send.at[n, 0], recv_sem=m_recv.at[n, yh, k],
                device_id=sib, device_id_type=MESH).start()

    wo_cp.wait()
    got = {}
    for n, d in enumerate(order):
        xx = (x + d) % 4
        for a in (0, 1):
            for j in (0, 1):
                ref = m.at[a, :, xx, :, pl.ds(j * 512, 512)]
                pltpu.make_async_copy(ref, ref, m_recv.at[n, a, j]).wait()

        def one(zz, carry):
            lhs = m[:, :, xx].reshape(256, 1024)
            o = jnp.dot(lhs, wo[zz], preferred_element_type=F32).astype(BF)
            part[d, :, :, pl.ds(pl.multiple_of(zz * 256, 256), 256)] = o.reshape(4, 64, 256)
            return carry
        lax.fori_loop(0, 8, one, 0)
        if d:
            for r in (2, 1, 3, 0):
                yy = flip(yh, RELS[r][0]) * 2 + flip(yl, RELS[r][1])
                got[d, r] = cps.go(part.at[d, yy], rx.at[d - 1, r], xdev(d))

    ysend = {}
    y_self = yh * 2 + yl
    for r in (2, 1, 3, 0):
        yy = flip(yh, RELS[r][0]) * 2 + flip(yl, RELS[r][1])
        for d in (2, 1, 3):
            got[d, r].wait_recv()
        total = part[0, yy].astype(F32)
        for d in (1, 2, 3):
            total += rx[d - 1, r].astype(F32)
        total = total.astype(BF)
        if r:
            slab[r - 1] = total
            ysend[r] = cps.go(slab.at[r - 1], ry.at[r - 1], ydev(RELS[r]))
        else:
            for zz in range(8):
                out[:, pl.ds(pl.multiple_of((zz * 4 + y_self) * 256, 256), 256)] = total[:, zz * 256:(zz + 1) * 256]
    for r in (2, 1, 3):
        yy = flip(yh, RELS[r][0]) * 2 + flip(yl, RELS[r][1])
        ysend[r].wait_recv()
        for zz in range(8):
            out[:, pl.ds(pl.multiple_of((zz * 4 + yy) * 256, 256), 256)] = ry[r - 1, :, zz * 256:(zz + 1) * 256]

    for cp in sends:
        cp.wait_send()

    @pl.when(k != yl)
    def _():
        for n, d in enumerate(order):
            xx = (x + d) % 4
            pltpu.make_async_remote_copy(
                src_ref=mixed.at[:, xx], dst_ref=m.at[yh, :, xx, :, pl.ds(pl.multiple_of(k * 512, 512), 512)],
                send_sem=m_send.at[n, 0], recv_sem=m_recv.at[n, yh, k],
                device_id=sib, device_id_type=MESH).wait_send()
    cps.finish()


V = pl.BlockSpec(memory_space=pltpu.VMEM)
ANY = pl.BlockSpec(memory_space=pl.ANY)
DMA = pltpu.SemaphoreType.DMA


def tables(segments):
    length = segments.shape[0]
    earlier = jnp.sum((segments[None, :] < segments[:, None]).astype(jnp.int32), axis=1)
    pos = (jnp.arange(length, dtype=jnp.int32) - earlier).astype(F32)
    freq = jnp.arange(HEAD // 2, dtype=F32)
    inverse = jnp.exp(freq * (-2.0 * math.log(500000.0) / HEAD))
    angles = pos[:, None] * inverse[None, :]
    c, s = jnp.cos(angles), jnp.sin(angles)
    return jnp.concatenate([c, c, -s, s, jnp.broadcast_to(pos[:, None], (length, 128))], axis=1)


def body(hidden, gain, segment_ids, w_query, key_matrix, value_matrix, w_out):
    tab = tables(segment_ids[0])
    qkv, tab2, wo_all = pl.pallas_call(
        project_kernel,
        out_shape=(jax.ShapeDtypeStruct((512, 768), F32), jax.ShapeDtypeStruct((512, 384), F32),
                   jax.ShapeDtypeStruct((8, 1024, 256), BF)),
        in_specs=[V, V, ANY, ANY, ANY, ANY, V],
        out_specs=(V, V, ANY),
        scratch_shapes=[
            pltpu.VMEM((3, 64, 2048), BF),
            pltpu.VMEM((4, 2, 4, 64, 2048), BF),
            pltpu.VMEM((2048, 512), BF),
            pltpu.VMEM((2048, 256), BF),
            pltpu.VMEM((4, 2, 256, 768), BF),
            pltpu.VMEM((3, 512, 768), BF),
            pltpu.VMEM((512, 384), F32),
            DMA((N_A + 20,)), DMA((N_A + 20,)), DMA((4,)), DMA((4,)), DMA((3,)),
        ],
        compiler_params=pltpu.CompilerParams(
            collective_id=0, has_side_effects=True, vmem_limit_bytes=VMEM_LIMIT),
        name="project",
    )(hidden, gain.reshape(1, -1), w_query, key_matrix, value_matrix, w_out, tab)
    mixed = pl.pallas_call(
        attend_kernel,
        out_shape=jax.ShapeDtypeStruct((512, 512), BF),
        in_specs=[V, V],
        out_specs=V,
        compiler_params=pltpu.CompilerParams(vmem_limit_bytes=VMEM_LIMIT),
        name="attend",
    )(qkv, tab2)
    return pl.pallas_call(
        output_kernel,
        out_shape=jax.ShapeDtypeStruct((64, 8192), BF),
        in_specs=[V, ANY],
        out_specs=V,
        scratch_shapes=[
            pltpu.VMEM((2, 2, 4, 64, 1024), BF),
            pltpu.VMEM((8, 1024, 256), BF),
            pltpu.VMEM((4, 4, 64, 2048), BF),
            pltpu.VMEM((3, 4, 64, 2048), BF),
            pltpu.VMEM((3, 64, 2048), BF),
            pltpu.VMEM((3, 64, 2048), BF),
            DMA((N_C,)), DMA((N_C,)), DMA((4, 4)), DMA((4, 2, 2)), DMA,
        ],
        compiler_params=pltpu.CompilerParams(
            collective_id=1, has_side_effects=True, vmem_limit_bytes=VMEM_LIMIT),
        name="output",
    )(mixed.reshape(2, 4, 64, 512), wo_all)


def solution(mesh):
    placed = (
        P(("dp", "tensor"), None), P(), P("dp", None), P("dp", "tensor"),
        P("dp", "tensor"), P("dp", "tensor"), P("tensor", "dp"),
    )
    return jax.shard_map(
        body, mesh=mesh, in_specs=placed, out_specs=P(("dp", "tensor"), None), check_vma=False)
```

```python
import math

import jax
import jax.numpy as jnp
from jax import lax
from jax.experimental import pallas as pl
from jax.experimental.pallas import tpu as pltpu
from jax.sharding import PartitionSpec as P

MESH = pl.DeviceIdType.MESH
BF = jnp.bfloat16
F32 = jnp.float32
HEAD = 128
VMEM_LIMIT = 56 * 2**20

RELS = ((0, 0), (1, 1), (1, 0), (0, 1))
SLOT = {r: i for i, r in enumerate(RELS)}
N_COPIES = 240


def place():
    dp = lax.axis_index("dp")
    t = lax.axis_index("tensor")
    return t % 4, (dp // 2) % 2, t // 4, dp // 4, dp % 2


def device(x, yh, yl, z, k):
    return (z * 4 + yh * 2 + k, yl * 4 + x)


def flip(v, f):
    return 1 - v if f else v


def at(start, size):
    return pl.ds(pl.multiple_of(start, size), size)


class Copies:
    def __init__(self, send, recv):
        self.send, self.recv, self.n, self.open = send, recv, 0, []

    def go(self, src, dst, dev, recv=None):
        i = self.n
        self.n += 1
        cp = pltpu.make_async_remote_copy(
            src_ref=src, dst_ref=dst, send_sem=self.send.at[i],
            recv_sem=self.recv.at[i] if recv is None else recv,
            device_id=dev, device_id_type=MESH)
        cp.start()
        self.open.append(cp)
        return cp

    def finish(self):
        for cp in self.open:
            cp.wait_send()


def kernel(hid_in, gain, seg, wq, wk, wv, wo_in, out,
           hid, xn, xs, w, wo, part, got, segs, qs, ks, vs, mixed, m, part2, fwd, rx, slab, ry,
           send, recv, hid_sem, swap_send, swap_recv, got_sem, m_send, m_recv, fwd_sem):
    x, yh, yl, z, k = place()
    y_self = yh * 2 + yl
    sib = device(x, yh, yl, z, 1 - k)
    swapped = device(x, yh, k, z, yl)
    cps = Copies(send, recv)

    def ydev(r):
        return device(x, flip(yh, r[0]), flip(yl, r[1]), z, k)

    def xdev(d):
        return device((x + d + 4) % 4, yh, yl, z, k)

    def zdev(d):
        return device(x, yh, yl, (z + d + 8) % 8, k)

    def mdev(r):
        return device(x, flip(yh, r[0]), flip(yl, r[1]), z, yl)

    hid_cp = pltpu.make_async_copy(hid_in, hid, hid_sem)
    hid_cp.start()

    bar = pltpu.get_barrier_semaphore()
    for dev in [ydev(r) for r in RELS[1:]] + [xdev(1), xdev(-1), zdev(1), zdev(-1), sib]:
        pl.semaphore_signal(bar, inc=1, device_id=dev, device_id_type=MESH)

    @pl.when(k != yl)
    def _():
        pl.semaphore_signal(bar, inc=1, device_id=swapped, device_id_type=MESH)

    for a in (0, 1):
        for j in (0, 1):
            src = device(x, flip(yh, a), k, z, j)
            if a == 0:
                @pl.when((k != yl) | (k != j))
                def _():
                    pl.semaphore_signal(bar, inc=1, device_id=src, device_id_type=MESH)
            else:
                pl.semaphore_signal(bar, inc=1, device_id=src, device_id_type=MESH)
    pl.semaphore_wait(bar, 11 + 2 * ((k + yl) % 2))

    rows = at(z * 256, 256)
    pieces = [
        (wk, w.at[0, rows, pl.ds(0, 128)]),
        (wv, w.at[0, rows, pl.ds(128, 128)]),
        (wq.at[:, pl.ds(0, 256)], w.at[1, rows, :]),
        (wq.at[:, pl.ds(256, 256)], w.at[2, rows, :]),
    ]
    wo_mine = wo.at[z, at(k * 512, 512), :]
    wo_theirs = wo.at[z, at(yl * 512, 512), :]

    def swap_copy(i):
        src, dst = pieces[i] if i < 4 else (wo_in, wo_theirs)
        return pltpu.make_async_remote_copy(
            src_ref=src, dst_ref=dst, send_sem=swap_send.at[i], recv_sem=swap_recv.at[i],
            device_id=swapped, device_id_type=MESH)

    def own_copy(i):
        src, dst = pieces[i] if i < 4 else (wo_in, wo_mine)
        return pltpu.make_async_copy(src, dst, swap_recv.at[i])

    def swap(*which):
        @pl.when(k != yl)
        def _():
            for i in which:
                swap_copy(i).start()

        @pl.when(k == yl)
        def _():
            for i in which:
                own_copy(i).start()

    def wait_swap(*which):
        for i in which:
            own_copy(i).wait()

    swap(0, 1)

    hid_cp.wait()
    total = jnp.zeros((64, 256), F32)
    for i in range(32):
        v = hid[:, i * 256:(i + 1) * 256].astype(F32)
        total += v * v
    inv = lax.rsqrt(jnp.sum(total, axis=-1, keepdims=True) * (1.0 / 8192) + 1e-5)

    def slice_norm(r, store):
        yy = flip(yh, r[0]) * 2 + flip(yl, r[1])
        for zz in range(8):
            cols = at((zz * 4 + yy) * 256, 256)
            store(zz, (hid[:, cols].astype(F32) * inv * gain[:, cols]).astype(BF))

    def put0(zz, v):
        xs[0, k, x, :, zz * 256:(zz + 1) * 256] = v
    slice_norm(RELS[0], put0)

    xg, xh, sibs, ysend = {}, {}, {}, {}

    def to_sib(r, d):
        ref = xs.at[r, k, (x - d + 4) % 4]
        sibs[r, d] = cps.go(ref, ref, sib)

    def spread(r):
        if r:
            ysend[r].wait_recv()
        ref = xs.at[r, k, x]
        for d in (1, -1):
            xg[r, d] = cps.go(ref, ref, xdev(d))
        to_sib(r, 0)

    def relay(r):
        for d in (1, -1):
            xg[r, d].wait_recv()
            ref = xs.at[r, k, (x - d + 4) % 4, pl.ds(0 if d == 1 else 32, 32)]
            xh[r, d] = cps.go(ref, ref, xdev(d))
            to_sib(r, d)

    def last(r):
        xh[r, 1].wait_recv()
        xh[r, -1].wait_recv()
        to_sib(r, 2)

    ring = {}

    def ring_ref(n, b, hf):
        if n < 3:
            return w.at[n, at(b * 256 + hf * 128, 128), :]
        return wo.at[b, at(k * 512 + hf * 256, 256), :]

    def share(b):
        ref = wo.at[b, at(k * 512, 512), :]
        shared.append(cps.go(ref, ref, sib))

    shared = []

    def ring_step(n, s):
        for hf in (0, 1):
            for d in (1, -1):
                if s > 0:
                    ring[n, s - 1, hf, d].wait_recv()
                if s == 3 and hf != (0 if d == 1 else 1):
                    continue
                ref = ring_ref(n, (z - d * s + 8) % 8, hf)
                ring[n, s, hf, d] = cps.go(ref, ref, zdev(d))
        if n == 3:
            share((z + s) % 8)
            if s:
                share((z - s + 8) % 8)

    def ring_end(n):
        ring[n, 3, 0, 1].wait_recv()
        ring[n, 3, 1, -1].wait_recv()
        if n == 3:
            share((z + 4) % 8)

    def scatter(r, rows_at, size, c0, width):
        a, b = RELS[r]
        for e in (1, 0):
            if (a, e) == (0, 0):
                continue
            slot = SLOT[(a, e)] - 1
            cps.go(part.at[r, flip(yl, e), rows_at, pl.ds(c0, width)],
                   got.at[slot, at(flip(yl, b) * 256 + rows_at.start, size), pl.ds(c0, width)],
                   ydev((a, e)), recv=got_sem.at[slot])

    def comp(r, g):
        def one(c, carry):
            part[r, c, :, g * 256:(g + 1) * 256] = jnp.dot(
                xs[r, c].reshape(256, 2048), w[g], preferred_element_type=F32).astype(BF)
            return carry
        lax.fori_loop(0, 2, one, 0)
        scatter(r, pl.ds(0, 256), 256, g * 256, 256)

    def comp_slab(r, d):
        xx = (x - d + 4) % 4
        lhs = xs[r, :, xx].reshape(128, 2048)

        def one(g, carry):
            o = jnp.dot(lhs, w[g], preferred_element_type=F32).astype(BF)
            part[r, :, at(xx * 64, 64), at(g * 256, 256)] = o.reshape(2, 64, 256)
            return carry
        lax.fori_loop(0, 3, one, 0)
        scatter(r, at(xx * 64, 64), 64, 0, 768)

    spread(0)
    wait_swap(0, 1)
    ring_step(0, 0)
    swap(2)
    for r in (1, 2, 3):
        def put(zz, v, r=r):
            xn[r - 1, :, zz * 256:(zz + 1) * 256] = v
        slice_norm(RELS[r], put)
        ysend[r] = cps.go(xn.at[r - 1], xs.at[r, k, x], ydev(RELS[r]))
    swap(3, 4)
    segs[0] = jnp.broadcast_to(seg[...].astype(F32), (8, 512))
    seg_cp = cps.go(segs.at[0], segs.at[1], sib)
    ring_step(0, 1)
    relay(0)
    ring_step(0, 2)
    spread(1)
    wait_swap(2)
    ring_step(1, 0)
    ring_step(0, 3)
    last(0)
    ring_end(0)
    ring_step(1, 1)
    for d in (0, 1, -1, 2):
        sibs[0, d].wait_recv()
    comp(0, 0)
    spread(2)
    relay(1)
    ring_step(1, 2)
    wait_swap(3)
    ring_step(2, 0)
    ring_step(1, 3)

    seg_cp.wait_recv()
    own_row = jnp.where(k == yl, segs[0, 0:1, :], segs[1, 0:1, :])
    i_col = lax.broadcasted_iota(jnp.int32, (512, 512), 0)
    i_row = lax.broadcasted_iota(jnp.int32, (512, 512), 1)
    seg_col = jnp.sum(jnp.where(i_col == i_row, own_row, 0.0), axis=1, keepdims=True)
    start = jnp.sum(jnp.where(own_row < seg_col, 1.0, 0.0), axis=1, keepdims=True)
    lane = lax.broadcasted_iota(jnp.int32, (1, HEAD), 1)
    freq = jnp.where(lane < 64, lane, lane - 64).astype(F32)
    inverse = jnp.exp(freq * (-2.0 * math.log(500000.0) / HEAD))
    pos = lax.broadcasted_iota(jnp.int32, (512, 1), 0).astype(F32) - start
    angles = pos * inverse
    cos = jnp.cos(angles)
    sin = jnp.where(lane < 64, -1.0, 1.0) * jnp.sin(angles)

    last(1)
    for d in (0, 1, -1, 2):
        sibs[1, d].wait_recv()
    comp(1, 0)
    ring_end(1)
    comp(0, 1)
    comp(1, 1)
    ring_step(2, 1)
    spread(3)
    relay(2)
    ring_step(2, 2)
    wait_swap(4)
    ring_step(3, 0)
    ring_step(2, 3)
    last(2)
    for d in (0, 1, -1, 2):
        sibs[2, d].wait_recv()
    comp(2, 0)
    comp(2, 1)
    ring_end(2)
    comp(2, 2)
    comp(1, 2)
    comp(0, 2)
    ring_step(3, 1)
    relay(3)
    for d in (0, 1, -1):
        sibs[3, d].wait_recv()
        comp_slab(3, d)
    ring_step(3, 2)
    last(3)
    sibs[3, 2].wait_recv()
    comp_slab(3, 2)
    ring_step(3, 3)

    def rotate(u):
        return (u * cos_b + pltpu.roll(u, 64, axis=1) * sin_b).astype(BF)

    for slot in range(3):
        pltpu.make_async_copy(got.at[slot], got.at[slot], got_sem.at[slot]).wait()
    for b in (0, 1):
        r = SLOT[(0, b)]
        half = flip(yl, b)
        rows_b = at(half * 256, 256)
        cos_b = jnp.where(half == 0, cos[0:256], cos[256:512])
        sin_b = jnp.where(half == 0, sin[0:256], sin[256:512])
        for i in range(6):
            cols = slice(i * 128, (i + 1) * 128)
            u = part[r, yl, :, cols].astype(F32)
            for slot in range(3):
                u += got[slot, rows_b, cols].astype(F32)
            if i == 0:
                ks[rows_b, :] = rotate(u)
            elif i == 1:
                vs[rows_b, :] = u.astype(BF)
            else:
                qs[rows_b, (i - 2) * 128:(i - 1) * 128] = rotate(u)

    scale = 1.0 / math.sqrt(HEAD)

    def attend(i):
        lo, hi = i * 128, (i + 1) * 128
        q = jnp.concatenate([qs[lo:hi, j * 128:(j + 1) * 128] for j in range(4)], axis=0)
        s = lax.dot_general(q, ks[:hi], (((1,), (1,)), ((), ())), preferred_element_type=F32) * scale
        where_i = lax.broadcasted_iota(jnp.int32, (128, hi), 0) + lo
        where_s = lax.broadcasted_iota(jnp.int32, (128, hi), 1)
        ok = (where_s <= where_i) & (where_s >= start[lo:hi].astype(jnp.int32))
        s = jnp.where(ok[None], s.reshape(4, 128, hi), -1e30)
        e = jnp.exp(s - jnp.max(s, axis=-1, keepdims=True))
        weights = (e / jnp.sum(e, axis=-1, keepdims=True)).astype(BF)
        o = jnp.dot(weights.reshape(512, hi), vs[:hi], preferred_element_type=F32).astype(BF)
        for j in range(4):
            for half in (0, 1):
                mixed[i // 2, (i % 2) * 2 + half, :, j * 128:(j + 1) * 128] = (
                    o[j * 128 + half * 64:j * 128 + half * 64 + 64])

    order = ((2, 0), (2, 1), (1, 0), (3, 0), (1, 1), (3, 1), (0, 0), (0, 1))

    def mixed_refs(n):
        d, l = order[n]
        xx = (x + d) % 4
        return mixed.at[l, xx], m.at[yh, l, xx, :, at(k * 512, 512)]

    def mixed_sib(n):
        src, dst = mixed_refs(n)
        return pltpu.make_async_remote_copy(
            src_ref=src, dst_ref=dst, send_sem=m_send.at[n], recv_sem=m_recv.at[n, yh, k],
            device_id=sib, device_id_type=MESH)

    def send_mixed(n):
        src, dst = mixed_refs(n)
        for r in (2, 1, 3):
            cps.go(src, dst, mdev(RELS[r]), recv=m_recv.at[n, yh, k])

        @pl.when(k == yl)
        def _():
            pltpu.make_async_copy(src, dst, m_recv.at[n, yh, k]).start()

        @pl.when(k != yl)
        def _():
            mixed_sib(n).start()

    attend(0)
    attend(1)
    send_mixed(0)
    attend(2)
    attend(3)
    for n in range(1, 8):
        send_mixed(n)
    ring_end(3)
    for cp in shared:
        cp.wait_recv()

    lo_cols, hi_cols = pl.ds(0, 1024), pl.ds(1024, 1024)

    def comp_out(n):
        d, l = order[n]
        xx = (x + d) % 4
        for a in (0, 1):
            for j in (0, 1):
                ref = m.at[a, l, xx, :, pl.ds(j * 512, 512)]
                pltpu.make_async_copy(ref, ref, m_recv.at[n, a, j]).wait()
        lhs = m[:, l, xx].reshape(128, 1024)

        def one(zz, carry):
            o = jnp.dot(lhs, wo[zz], preferred_element_type=F32).astype(BF)
            part2[d, :, l, :, at(zz * 256, 256)] = o.reshape(2, 64, 256)
            return carry
        lax.fori_loop(0, 8, one, 0)

    for n in (0, 1):
        comp_out(n)
        l = order[n][1]
        for a in (0, 1):
            cps.go(part2.at[2, a, l, :, hi_cols], fwd.at[0, a, l], xdev(1), recv=fwd_sem.at[0, a, l])
            cps.go(part2.at[2, a, l, :, lo_cols], fwd.at[1, a, l], xdev(-1), recv=fwd_sem.at[1, a, l])
    for n in range(2, 6):
        comp_out(n)

    alone, summed = {}, {}
    rel_order = (2, 1, 3, 0)

    def slab_at(r):
        return flip(yh, RELS[r][0]), flip(yl, RELS[r][1])

    for r in rel_order:
        a, l = slab_at(r)
        alone[r, 1] = cps.go(part2.at[1, a, l, :, lo_cols], rx.at[0, r, :, lo_cols], xdev(1))
        alone[r, -1] = cps.go(part2.at[3, a, l, :, hi_cols], rx.at[1, r, :, hi_cols], xdev(-1))
        for i, d, cols in ((0, 1, slice(1024, 2048)), (1, -1, slice(0, 1024))):
            ref = fwd.at[i, a, l]
            pltpu.make_async_copy(ref, ref, fwd_sem.at[i, a, l]).wait()
            part2[d % 4, a, l, :, cols] = (
                part2[d % 4, a, l, :, cols].astype(F32) + fwd[i, a, l].astype(F32)).astype(BF)
            pcols = pl.ds(cols.start, 1024)
            summed[r, d] = cps.go(part2.at[d % 4, a, l, :, pcols], rx.at[i, r, :, pcols], xdev(d))
    for n in (6, 7):
        comp_out(n)

    last_send = {}
    for r in rel_order:
        a, l = slab_at(r)
        for d in (1, -1):
            alone[r, d].wait_recv()
            summed[r, d].wait_recv()
        o = (part2[0, a, l].astype(F32) + rx[0, r].astype(F32) + rx[1, r].astype(F32)).astype(BF)
        if r:
            slab[r - 1] = o
            last_send[r] = cps.go(slab.at[r - 1], ry.at[r - 1], ydev(RELS[r]))
        else:
            for zz in range(8):
                out[:, at((zz * 4 + y_self) * 256, 256)] = o[:, zz * 256:(zz + 1) * 256]
    for r in (2, 1, 3):
        a, l = slab_at(r)
        last_send[r].wait_recv()
        for zz in range(8):
            out[:, at((zz * 4 + a * 2 + l) * 256, 256)] = ry[r - 1, :, zz * 256:(zz + 1) * 256]

    @pl.when(k != yl)
    def _():
        for i in range(5):
            swap_copy(i).wait_send()
        for n in range(8):
            mixed_sib(n).wait_send()
    cps.finish()


V = pl.BlockSpec(memory_space=pltpu.VMEM)
ANY = pl.BlockSpec(memory_space=pl.ANY)
DMA = pltpu.SemaphoreType.DMA


def body(hidden, gain, segment_ids, w_query, key_matrix, value_matrix, w_out):
    return pl.pallas_call(
        kernel,
        out_shape=jax.ShapeDtypeStruct((64, 8192), BF),
        in_specs=[ANY, V, V, ANY, ANY, ANY, ANY],
        out_specs=V,
        scratch_shapes=[
            pltpu.VMEM((64, 8192), BF),
            pltpu.VMEM((3, 64, 2048), BF),
            pltpu.VMEM((4, 2, 4, 64, 2048), BF),
            pltpu.VMEM((3, 2048, 256), BF),
            pltpu.VMEM((8, 1024, 256), BF),
            pltpu.VMEM((4, 2, 256, 768), BF),
            pltpu.VMEM((3, 512, 768), BF),
            pltpu.VMEM((2, 8, 512), F32),
            pltpu.VMEM((512, 512), BF),
            pltpu.VMEM((512, 128), BF),
            pltpu.VMEM((512, 128), BF),
            pltpu.VMEM((2, 4, 64, 512), BF),
            pltpu.VMEM((2, 2, 4, 64, 1024), BF),
            pltpu.VMEM((4, 2, 2, 64, 2048), BF),
            pltpu.VMEM((2, 2, 2, 64, 1024), BF),
            pltpu.VMEM((2, 4, 64, 2048), BF),
            pltpu.VMEM((3, 64, 2048), BF),
            pltpu.VMEM((3, 64, 2048), BF),
            DMA((N_COPIES,)), DMA((N_COPIES,)), DMA, DMA((5,)), DMA((5,)), DMA((3,)),
            DMA((8,)), DMA((8, 2, 2)), DMA((2, 2, 2)),
        ],
        compiler_params=pltpu.CompilerParams(
            collective_id=0, has_side_effects=True, vmem_limit_bytes=VMEM_LIMIT),
        name="sublayer",
    )(hidden, gain.reshape(1, -1), segment_ids, w_query, key_matrix, value_matrix, w_out)


def solution(mesh):
    placed = (
        P(("dp", "tensor"), None), P(), P("dp", None), P("dp", "tensor"),
        P("dp", "tensor"), P("dp", "tensor"), P("tensor", "dp"),
    )
    return jax.shard_map(
        body, mesh=mesh, in_specs=placed, out_specs=P(("dp", "tensor"), None), check_vma=False)
```

```python
import math

import jax
import jax.numpy as jnp
from jax import lax
from jax.experimental import pallas as pl
from jax.experimental.pallas import tpu as pltpu
from jax.sharding import PartitionSpec as P

MESH = pl.DeviceIdType.MESH
BF = jnp.bfloat16
F32 = jnp.float32
HEAD = 128
VMEM_LIMIT = 56 * 2**20

RELS = ((0, 0), (1, 1), (1, 0), (0, 1))
SLOT = {r: i for i, r in enumerate(RELS)}
N_COPIES = 240


def place():
    dp = lax.axis_index("dp")
    t = lax.axis_index("tensor")
    return t % 4, (dp // 2) % 2, t // 4, dp // 4, dp % 2


def device(x, yh, yl, z, k):
    return (z * 4 + yh * 2 + k, yl * 4 + x)


def flip(v, f):
    return 1 - v if f else v


def at(start, size):
    return pl.ds(pl.multiple_of(start, size), size)


class Copies:
    def __init__(self, send, recv):
        self.send, self.recv, self.n, self.open = send, recv, 0, []

    def go(self, src, dst, dev, recv=None):
        i = self.n
        self.n += 1
        cp = pltpu.make_async_remote_copy(
            src_ref=src, dst_ref=dst, send_sem=self.send.at[i],
            recv_sem=self.recv.at[i] if recv is None else recv,
            device_id=dev, device_id_type=MESH)
        cp.start()
        self.open.append(cp)
        return cp

    def finish(self):
        for cp in self.open:
            cp.wait_send()


def kernel(hid_in, gain, seg, wq, wk, wv, wo_in, out,
           hid, xn, xs, w, wo, part, got, fa, fb, segs, qs, ks, vs, mixed, m, part2, fwd, rx, slab, ry,
           send, recv, hid_sem, swap_send, swap_recv, got_sem, m_send, m_recv, fwd_sem):
    x, yh, yl, z, k = place()
    y_self = yh * 2 + yl
    sib = device(x, yh, yl, z, 1 - k)
    swapped = device(x, yh, k, z, yl)
    cps = Copies(send, recv)

    def ydev(r):
        return device(x, flip(yh, r[0]), flip(yl, r[1]), z, k)

    def xdev(d):
        return device((x + d + 4) % 4, yh, yl, z, k)

    def zdev(d):
        return device(x, yh, yl, (z + d + 8) % 8, k)

    def mdev(r):
        return device(x, flip(yh, r[0]), flip(yl, r[1]), z, yl)

    hid_cp = pltpu.make_async_copy(hid_in, hid, hid_sem)
    hid_cp.start()

    bar = pltpu.get_barrier_semaphore()
    for dev in [ydev(r) for r in RELS[1:]] + [xdev(1), xdev(-1), zdev(1), zdev(-1), sib]:
        pl.semaphore_signal(bar, inc=1, device_id=dev, device_id_type=MESH)

    @pl.when(k != yl)
    def _():
        pl.semaphore_signal(bar, inc=1, device_id=swapped, device_id_type=MESH)

    for a in (0, 1):
        for j in (0, 1):
            src = device(x, flip(yh, a), k, z, j)
            if a == 0:
                @pl.when((k != yl) | (k != j))
                def _():
                    pl.semaphore_signal(bar, inc=1, device_id=src, device_id_type=MESH)
            else:
                pl.semaphore_signal(bar, inc=1, device_id=src, device_id_type=MESH)
    pl.semaphore_wait(bar, 11 + 2 * ((k + yl) % 2))

    rows = at(z * 256, 256)
    pieces = [
        (wk, w.at[0, rows, pl.ds(0, 128)]),
        (wv, w.at[0, rows, pl.ds(128, 128)]),
        (wq.at[:, pl.ds(0, 256)], w.at[1, rows, :]),
        (wq.at[:, pl.ds(256, 256)], w.at[2, rows, :]),
    ]
    wo_mine = wo.at[z, at(k * 512, 512), :]
    wo_theirs = wo.at[z, at(yl * 512, 512), :]

    def swap_copy(i):
        src, dst = pieces[i] if i < 4 else (wo_in, wo_theirs)
        return pltpu.make_async_remote_copy(
            src_ref=src, dst_ref=dst, send_sem=swap_send.at[i], recv_sem=swap_recv.at[i],
            device_id=swapped, device_id_type=MESH)

    def own_copy(i):
        src, dst = pieces[i] if i < 4 else (wo_in, wo_mine)
        return pltpu.make_async_copy(src, dst, swap_recv.at[i])

    groups = ((0, 1), (2,), (3,), (4,))

    def swap(group):
        which = groups[group]

        @pl.when(k != yl)
        def _():
            for i in which:
                swap_copy(i).start()

        @pl.when(k == yl)
        def _():
            for i in which:
                own_copy(i).start()

    def wait_swap(group):
        for i in groups[group]:
            own_copy(i).wait()

    swap(0)

    hid_cp.wait()
    total = jnp.zeros((64, 256), F32)
    for i in range(32):
        v = hid[:, i * 256:(i + 1) * 256].astype(F32)
        total += v * v
    inv = lax.rsqrt(jnp.sum(total, axis=-1, keepdims=True) * (1.0 / 8192) + 1e-5)

    def slice_norm(r, store):
        yy = flip(yh, r[0]) * 2 + flip(yl, r[1])
        for zz in range(8):
            cols = at((zz * 4 + yy) * 256, 256)
            store(zz, (hid[:, cols].astype(F32) * inv * gain[:, cols]).astype(BF))

    def put0(zz, v):
        xs[0, k, x, :, zz * 256:(zz + 1) * 256] = v

    def put_norm(r):
        def put(zz, v):
            xn[r - 1, :, zz * 256:(zz + 1) * 256] = v
        slice_norm(RELS[r], put)

    xg, xh, sibs, ysend = {}, {}, {}, {}

    def to_sib(r, d):
        ref = xs.at[r, k, (x - d + 4) % 4]
        sibs[r, d] = cps.go(ref, ref, sib)

    def spread(r):
        if r:
            ysend[r].wait_recv()
        ref = xs.at[r, k, x]
        for d in (1, -1):
            xg[r, d] = cps.go(ref, ref, xdev(d))
        to_sib(r, 0)

    def relay(r, d):
        xg[r, d].wait_recv()
        ref = xs.at[r, k, (x - d + 4) % 4, pl.ds(0 if d == 1 else 32, 32)]
        xh[r, d] = cps.go(ref, ref, xdev(d))
        to_sib(r, d)

    def last(r):
        xh[r, 1].wait_recv()
        xh[r, -1].wait_recv()
        to_sib(r, 2)

    ring = {}

    def ring_ref(n, b, hf):
        if n < 3:
            return w.at[n, at(b * 256 + hf * 128, 128), :]
        return wo.at[b, at(k * 512 + hf * 256, 256), :]

    def share(b):
        ref = wo.at[b, at(k * 512, 512), :]
        shared.append(cps.go(ref, ref, sib))

    shared = []

    def ring_half(n, s, hf):
        for d in (1, -1):
            if s > 0:
                ring[n, s - 1, hf, d].wait_recv()
            if s == 3 and hf != (0 if d == 1 else 1):
                continue
            ref = ring_ref(n, (z - d * s + 8) % 8, hf)
            ring[n, s, hf, d] = cps.go(ref, ref, zdev(d))
        if n == 3 and hf == 1:
            share((z + s) % 8)
            if s:
                share((z - s + 8) % 8)

    def ring_step(n, s):
        ring_half(n, s, 0)
        ring_half(n, s, 1)

    def ring_end(n):
        ring[n, 3, 0, 1].wait_recv()
        ring[n, 3, 1, -1].wait_recv()
        if n == 3:
            share((z + 4) % 8)

    far_a, far_b = {}, {}
    near, pair = RELS[1], RELS[3]
    low, high = pl.ds(0, 32), pl.ds(32, 32)

    def send_sum(r, xx, half, cols):
        a, b = RELS[r]
        slot = 0 if a else 1
        cps.go(part.at[r, 1 - yl, xx, half, cols], got.at[slot, flip(yl, b), xx, half, cols],
               ydev(near if a else pair), recv=got_sem.at[slot])

    def comp(r, g):
        a, b = RELS[r]
        cols = pl.ds(g * 256, 256)

        def one(c, carry):
            o = jnp.dot(xs[r, c].reshape(256, 2048), w[g], preferred_element_type=F32)
            part[r, c, :, :, g * 256:(g + 1) * 256] = o.astype(BF).reshape(4, 64, 256)
            return carry
        lax.fori_loop(0, 2, one, 0)
        if a:
            far_a[b, g] = cps.go(part.at[r, yl, :, low, cols], fa.at[1 - b, :, :, cols], ydev(pair))
            far_b[b, g] = cps.go(part.at[r, yl, :, high, cols], fb.at[1 - b, :, :, cols], ydev(near))
            send_sum(r, slice(None), high, cols)
        else:
            send_sum(r, slice(None), low, cols)

    def comp_slab(r, d):
        xx = (x - d + 4) % 4
        lhs = xs[r, :, xx].reshape(128, 2048)

        def one(g, carry):
            o = jnp.dot(lhs, w[g], preferred_element_type=F32).astype(BF)
            part[r, :, xx, :, at(g * 256, 256)] = o.reshape(2, 64, 256)
            return carry
        lax.fori_loop(0, 3, one, 0)
        send_sum(r, xx, low, slice(None))

    folded = set()

    def fold(r, i):
        a, b = RELS[r]
        far, buf, half, rows32 = (far_a, fa, low, slice(0, 32)) if a else (far_b, fb, high, slice(32, 64))
        slabs = r == 3
        for g in range(3) if slabs else (i,):
            if (r, g) not in folded:
                folded.add((r, g))
                far[1 - b, g].wait_recv()
        if slabs:
            xx, cols = (x - i + 4) % 4, slice(0, 768)
            part[r, 1 - yl, xx, rows32, cols] = (
                part[r, 1 - yl, xx, rows32, cols].astype(F32) + buf[b, xx].astype(F32)).astype(BF)
            send_sum(r, xx, half, slice(None))
        else:
            cols = slice(i * 256, (i + 1) * 256)
            part[r, 1 - yl, :, rows32, cols] = (
                part[r, 1 - yl, :, rows32, cols].astype(F32) + buf[b, :, :, cols].astype(F32)).astype(BF)
            send_sum(r, slice(None), half, pl.ds(i * 256, 256))

    def send_slice(r):
        ysend[r] = cps.go(xn.at[r - 1], xs.at[r, k, x], ydev(RELS[r]))

    def wait_sib(r):
        for d in (0, 1, -1, 2):
            sibs[r, d].wait_recv()

    tab = {}

    def tables():
        seg_cp.wait_recv()
        own_row = jnp.where(k == yl, segs[0, 0:1, :], segs[1, 0:1, :])
        i_col = lax.broadcasted_iota(jnp.int32, (512, 512), 0)
        i_row = lax.broadcasted_iota(jnp.int32, (512, 512), 1)
        seg_col = jnp.sum(jnp.where(i_col == i_row, own_row, 0.0), axis=1, keepdims=True)
        start = jnp.sum(jnp.where(own_row < seg_col, 1.0, 0.0), axis=1, keepdims=True)
        lane = lax.broadcasted_iota(jnp.int32, (1, HEAD), 1)
        freq = jnp.where(lane < 64, lane, lane - 64).astype(F32)
        inverse = jnp.exp(freq * (-2.0 * math.log(500000.0) / HEAD))
        pos = lax.broadcasted_iota(jnp.int32, (512, 1), 0).astype(F32) - start
        angles = pos * inverse
        cos = jnp.cos(angles)
        sin = jnp.where(lane < 64, -1.0, 1.0) * jnp.sin(angles)
        tab.update(start=start, cos=cos, sin=sin)

    put_norm(1)
    send_slice(1)
    slice_norm(RELS[0], put0)
    spread(0)
    swap(1)
    put_norm(2)
    put_norm(3)
    segs[0] = jnp.broadcast_to(seg[...].astype(F32), (8, 512))
    seg_cp = cps.go(segs.at[0], segs.at[1], sib)

    wait_swap(0)
    ring_half(0, 0, 0)
    ring_half(0, 0, 1)
    wait_swap(1)
    ring_half(1, 0, 0)
    ring_half(1, 0, 1)
    swap(2)
    ring_half(0, 1, 0)
    spread(1)
    send_slice(2)
    relay(0, -1)
    relay(0, 1)
    ring_half(0, 1, 1)
    wait_swap(2)
    ring_half(2, 0, 0)
    ring_half(2, 0, 1)
    swap(3)
    ring_half(1, 1, 0)
    ring_half(1, 1, 1)
    ring_half(0, 2, 0)
    ring_half(0, 2, 1)
    ring_half(2, 1, 0)
    relay(1, -1)
    relay(1, 1)
    spread(2)
    send_slice(3)
    ring_half(2, 1, 1)
    ring_half(1, 2, 0)
    last(0)
    tables()
    ring_half(1, 2, 1)
    ring_half(0, 3, 0)
    last(1)
    ring_half(0, 3, 1)
    ring_half(2, 2, 0)
    spread(3)
    ring_half(2, 2, 1)
    ring_half(1, 3, 0)
    relay(2, -1)
    relay(2, 1)
    ring_half(1, 3, 1)
    wait_sib(1)
    ring_end(0)
    comp(1, 0)
    wait_sib(0)
    comp(0, 0)
    ring_half(2, 3, 0)
    ring_half(2, 3, 1)
    wait_swap(3)
    ring_half(3, 0, 0)
    ring_half(3, 0, 1)
    relay(3, -1)
    relay(3, 1)
    ring_end(1)
    comp(1, 1)
    fold(0, 0)
    comp(0, 1)
    last(2)
    ring_end(2)
    comp(1, 2)
    comp(0, 2)
    wait_sib(2)
    comp(2, 0)
    last(3)
    fold(0, 1)
    fold(2, 0)
    ring_half(3, 1, 0)
    comp(2, 1)
    fold(2, 1)
    comp(2, 2)
    sibs[3, -1].wait_recv()
    comp_slab(3, -1)
    fold(0, 2)
    ring_half(3, 1, 1)
    sibs[3, 0].wait_recv()
    comp_slab(3, 0)
    fold(2, 2)
    sibs[3, 1].wait_recv()
    comp_slab(3, 1)
    sibs[3, 2].wait_recv()
    comp_slab(3, 2)
    ring_half(3, 2, 0)
    fold(1, 0)
    ring_half(3, 2, 1)
    fold(1, 1)
    fold(1, 2)
    ring_half(3, 3, 0)
    fold(3, -1)
    fold(3, 0)
    fold(3, 1)
    fold(3, 2)
    ring_half(3, 3, 1)

    def rotate(u):
        return (u * cos_b + pltpu.roll(u, 64, axis=1) * sin_b).astype(BF)

    start, cos, sin = tab["start"], tab["cos"], tab["sin"]
    for slot in range(2):
        pltpu.make_async_copy(got.at[slot], got.at[slot], got_sem.at[slot]).wait()
    for b in (0, 1):
        r = SLOT[(0, b)]
        half = flip(yl, b)
        rows_b = at(half * 256, 256)
        cos_b = jnp.where(half == 0, cos[0:256], cos[256:512])
        sin_b = jnp.where(half == 0, sin[0:256], sin[256:512])
        for i in range(6):
            cols = slice(i * 128, (i + 1) * 128)
            u = part[r, yl, :, :, cols].astype(F32)
            for slot in range(2):
                u += got[slot, half, :, :, cols].astype(F32)
            u = u.reshape(256, 128)
            if i == 0:
                ks[rows_b, :] = rotate(u)
            elif i == 1:
                vs[rows_b, :] = u.astype(BF)
            else:
                qs[rows_b, (i - 2) * 128:(i - 1) * 128] = rotate(u)

    scale = 1.0 / math.sqrt(HEAD)

    def attend(i):
        lo, hi = i * 128, (i + 1) * 128
        q = jnp.concatenate([qs[lo:hi, j * 128:(j + 1) * 128] for j in range(4)], axis=0)
        s = lax.dot_general(q, ks[:hi], (((1,), (1,)), ((), ())), preferred_element_type=F32) * scale
        where_i = lax.broadcasted_iota(jnp.int32, (128, hi), 0) + lo
        where_s = lax.broadcasted_iota(jnp.int32, (128, hi), 1)
        ok = (where_s <= where_i) & (where_s >= start[lo:hi].astype(jnp.int32))
        s = jnp.where(ok[None], s.reshape(4, 128, hi), -1e30)
        e = jnp.exp(s - jnp.max(s, axis=-1, keepdims=True))
        weights = (e / jnp.sum(e, axis=-1, keepdims=True)).astype(BF)
        o = jnp.dot(weights.reshape(512, hi), vs[:hi], preferred_element_type=F32).astype(BF)
        for j in range(4):
            for half in (0, 1):
                mixed[i // 2, (i % 2) * 2 + half, :, j * 128:(j + 1) * 128] = (
                    o[j * 128 + half * 64:j * 128 + half * 64 + 64])

    order = ((2, 0), (2, 1), (1, 0), (3, 0), (1, 1), (3, 1), (0, 0), (0, 1))

    def mixed_refs(n, r):
        d, f = order[n]
        xx = (x + d) % 4
        l = flip(flip(yl, RELS[r][1]), f)
        return mixed.at[l, xx], m.at[yh, l, xx, :, at(k * 512, 512)]

    def mixed_sib(n):
        src, dst = mixed_refs(n, 0)
        return pltpu.make_async_remote_copy(
            src_ref=src, dst_ref=dst, send_sem=m_send.at[n], recv_sem=m_recv.at[n, yh, k],
            device_id=sib, device_id_type=MESH)

    def send_mixed(n):
        for r in (2, 1, 3):
            src, dst = mixed_refs(n, r)
            cps.go(src, dst, mdev(RELS[r]), recv=m_recv.at[n, yh, k])

        @pl.when(k == yl)
        def _():
            src, dst = mixed_refs(n, 0)
            pltpu.make_async_copy(src, dst, m_recv.at[n, yh, k]).start()

        @pl.when(k != yl)
        def _():
            mixed_sib(n).start()

    for i in range(4):
        attend(i)
    for n in range(8):
        send_mixed(n)
    ring_end(3)
    for cp in shared:
        cp.wait_recv()

    lo_cols, hi_cols = pl.ds(0, 1024), pl.ds(1024, 1024)

    def comp_out(n):
        d, f = order[n]
        l = flip(yl, f)
        xx = (x + d) % 4
        for a in (0, 1):
            for j in (0, 1):
                ref = m.at[a, l, xx, :, pl.ds(j * 512, 512)]
                pltpu.make_async_copy(ref, ref, m_recv.at[n, a, j]).wait()
        lhs = m[:, l, xx].reshape(128, 1024)

        def one(zz, carry):
            o = jnp.dot(lhs, wo[zz], preferred_element_type=F32).astype(BF)
            part2[d, :, l, :, at(zz * 256, 256)] = o.reshape(2, 64, 256)
            return carry
        lax.fori_loop(0, 8, one, 0)
        if d == 2:
            for a in (0, 1):
                cps.go(part2.at[2, a, l, :, hi_cols], fwd.at[0, a, l], xdev(1), recv=fwd_sem.at[0, a, l])
                cps.go(part2.at[2, a, l, :, lo_cols], fwd.at[1, a, l], xdev(-1), recv=fwd_sem.at[1, a, l])

    alone, summed = {}, {}
    rel_order = (2, 1, 3, 0)

    def slab_at(r):
        return flip(yh, RELS[r][0]), flip(yl, RELS[r][1])

    def send_slab(r):
        a, l = slab_at(r)
        alone[r, 1] = cps.go(part2.at[1, a, l, :, lo_cols], rx.at[0, r, :, lo_cols], xdev(1))
        alone[r, -1] = cps.go(part2.at[3, a, l, :, hi_cols], rx.at[1, r, :, hi_cols], xdev(-1))
        for i, d, cols in ((0, 1, slice(1024, 2048)), (1, -1, slice(0, 1024))):
            ref = fwd.at[i, a, l]
            pltpu.make_async_copy(ref, ref, fwd_sem.at[i, a, l]).wait()
            part2[d % 4, a, l, :, cols] = (
                part2[d % 4, a, l, :, cols].astype(F32) + fwd[i, a, l].astype(F32)).astype(BF)
            pcols = pl.ds(cols.start, 1024)
            summed[r, d] = cps.go(part2.at[d % 4, a, l, :, pcols], rx.at[i, r, :, pcols], xdev(d))

    for n in range(4):
        comp_out(n)
    send_slab(2)
    for n in range(4, 6):
        comp_out(n)
    for r in (1, 3, 0):
        send_slab(r)
    for n in (6, 7):
        comp_out(n)

    last_send = {}
    for r in rel_order:
        a, l = slab_at(r)
        for d in (1, -1):
            alone[r, d].wait_recv()
            summed[r, d].wait_recv()
        o = (part2[0, a, l].astype(F32) + rx[0, r].astype(F32) + rx[1, r].astype(F32)).astype(BF)
        if r:
            slab[r - 1] = o
            last_send[r] = cps.go(slab.at[r - 1], ry.at[r - 1], ydev(RELS[r]))
        else:
            for zz in range(8):
                out[:, at((zz * 4 + y_self) * 256, 256)] = o[:, zz * 256:(zz + 1) * 256]
    for r in (2, 1, 3):
        a, l = slab_at(r)
        last_send[r].wait_recv()
        for zz in range(8):
            out[:, at((zz * 4 + a * 2 + l) * 256, 256)] = ry[r - 1, :, zz * 256:(zz + 1) * 256]

    @pl.when(k != yl)
    def _():
        for i in range(5):
            swap_copy(i).wait_send()
        for n in range(8):
            mixed_sib(n).wait_send()
    cps.finish()


V = pl.BlockSpec(memory_space=pltpu.VMEM)
ANY = pl.BlockSpec(memory_space=pl.ANY)
DMA = pltpu.SemaphoreType.DMA


def body(hidden, gain, segment_ids, w_query, key_matrix, value_matrix, w_out):
    return pl.pallas_call(
        kernel,
        out_shape=jax.ShapeDtypeStruct((64, 8192), BF),
        in_specs=[ANY, V, V, ANY, ANY, ANY, ANY],
        out_specs=V,
        scratch_shapes=[
            pltpu.VMEM((64, 8192), BF),
            pltpu.VMEM((3, 64, 2048), BF),
            pltpu.VMEM((4, 2, 4, 64, 2048), BF),
            pltpu.VMEM((3, 2048, 256), BF),
            pltpu.VMEM((8, 1024, 256), BF),
            pltpu.VMEM((4, 2, 4, 64, 768), BF),
            pltpu.VMEM((2, 2, 4, 64, 768), BF),
            pltpu.VMEM((2, 4, 32, 768), BF),
            pltpu.VMEM((2, 4, 32, 768), BF),
            pltpu.VMEM((2, 8, 512), F32),
            pltpu.VMEM((512, 512), BF),
            pltpu.VMEM((512, 128), BF),
            pltpu.VMEM((512, 128), BF),
            pltpu.VMEM((2, 4, 64, 512), BF),
            pltpu.VMEM((2, 2, 4, 64, 1024), BF),
            pltpu.VMEM((4, 2, 2, 64, 2048), BF),
            pltpu.VMEM((2, 2, 2, 64, 1024), BF),
            pltpu.VMEM((2, 4, 64, 2048), BF),
            pltpu.VMEM((3, 64, 2048), BF),
            pltpu.VMEM((3, 64, 2048), BF),
            DMA((N_COPIES,)), DMA((N_COPIES,)), DMA, DMA((5,)), DMA((5,)), DMA((2,)),
            DMA((8,)), DMA((8, 2, 2)), DMA((2, 2, 2)),
        ],
        compiler_params=pltpu.CompilerParams(
            collective_id=0, has_side_effects=True, vmem_limit_bytes=VMEM_LIMIT),
        name="sublayer",
    )(hidden, gain.reshape(1, -1), segment_ids, w_query, key_matrix, value_matrix, w_out)


def solution(mesh):
    placed = (
        P(("dp", "tensor"), None), P(), P("dp", None), P("dp", "tensor"),
        P("dp", "tensor"), P("dp", "tensor"), P("tensor", "dp"),
    )
    return jax.shard_map(
        body, mesh=mesh, in_specs=placed, out_specs=P(("dp", "tensor"), None), check_vma=False)
```

```python
import math

import jax
import jax.numpy as jnp
from jax import lax
from jax.experimental import pallas as pl
from jax.experimental.pallas import tpu as pltpu
from jax.sharding import PartitionSpec as P

MESH = pl.DeviceIdType.MESH
BF = jnp.bfloat16
F32 = jnp.float32
HEAD = 128
VMEM_LIMIT = 56 * 2**20

RELS = ((0, 0), (1, 1), (1, 0), (0, 1))
SLOT = {r: i for i, r in enumerate(RELS)}


def place():
    dp = lax.axis_index("dp")
    t = lax.axis_index("tensor")
    return t % 4, (dp // 2) % 2, t // 4, dp // 4, dp % 2


def device(x, yh, yl, z, k):
    return (z * 4 + yh * 2 + k, yl * 4 + x)


def flip(v, f):
    return 1 - v if f else v


def at(start, size):
    return pl.ds(pl.multiple_of(start, size), size)


SENDS = ("ring0", "ring1", "ring2", "ring3", "spread", "relay", "sib", "slice", "seg", "far0", "far1", "sum0", "sum1",
         "mixed1", "mixed2", "mixed3", "share", "fwd", "cross", "last")


def wait(ref, sem):
    pltpu.make_async_copy(ref, ref, sem).wait()


def kernel(hid_in, gain, seg, wq, wk, wv, wo_in, out,
           hid, xn, xs, w, wo, part, got, fa, fb, segs, qs, ks, vs, mixed, m, part2, fwd, rx, slab,
           send, hid_sem, seg_sem, swap_send, swap_recv, y_recv, xg_recv, xh_recv, sib_recv, last_sib_recv,
           ring_recv, far_recv, share_recv, got_recv, m_send, m_recv, fwd_recv, cross_recv, last_recv):
    x, yh, yl, z, k = place()
    y_self = yh * 2 + yl
    sib = device(x, yh, yl, z, 1 - k)
    swapped = device(x, yh, k, z, yl)

    def go(name, src, dst, dev, recv):
        pltpu.make_async_remote_copy(
            src_ref=src, dst_ref=dst, send_sem=send.at[SENDS.index(name)], recv_sem=recv,
            device_id=dev, device_id_type=MESH).start()

    def ydev(r):
        return device(x, flip(yh, r[0]), flip(yl, r[1]), z, k)

    def xdev(d):
        return device((x + d + 4) % 4, yh, yl, z, k)

    def zdev(d):
        return device(x, yh, yl, (z + d + 8) % 8, k)

    def mdev(r):
        return device(x, flip(yh, r[0]), flip(yl, r[1]), z, yl)

    hid_cp = pltpu.make_async_copy(hid_in, hid, hid_sem)
    hid_cp.start()

    bar = pltpu.get_barrier_semaphore()
    for dev in [ydev(r) for r in RELS[1:]] + [xdev(1), xdev(-1), zdev(1), zdev(-1), sib]:
        pl.semaphore_signal(bar, inc=1, device_id=dev, device_id_type=MESH)

    @pl.when(k != yl)
    def _():
        pl.semaphore_signal(bar, inc=1, device_id=swapped, device_id_type=MESH)

    for a in (0, 1):
        for j in (0, 1):
            src = device(x, flip(yh, a), k, z, j)
            if a == 0:
                @pl.when((k != yl) | (k != j))
                def _():
                    pl.semaphore_signal(bar, inc=1, device_id=src, device_id_type=MESH)
            else:
                pl.semaphore_signal(bar, inc=1, device_id=src, device_id_type=MESH)
    pl.semaphore_wait(bar, 11 + 2 * ((k + yl) % 2))

    rows = at(z * 256, 256)
    pieces = [
        (wk, w.at[0, rows, pl.ds(0, 128)]),
        (wv, w.at[0, rows, pl.ds(128, 128)]),
        (wq.at[:, pl.ds(0, 256)], w.at[1, rows, :]),
        (wq.at[:, pl.ds(256, 256)], w.at[2, rows, :]),
    ]
    wo_mine = wo.at[z, at(k * 512, 512), :]
    wo_theirs = wo.at[z, at(yl * 512, 512), :]

    groups = ((0, 1), (2,), (3,), (4,))

    def swap(group):
        @pl.when(k != yl)
        def _():
            for i in groups[group]:
                src, dst = pieces[i] if i < 4 else (wo_in, wo_theirs)
                pltpu.make_async_remote_copy(
                    src_ref=src, dst_ref=dst, send_sem=swap_send, recv_sem=swap_recv.at[group],
                    device_id=swapped, device_id_type=MESH).start()

        @pl.when(k == yl)
        def _():
            for i in groups[group]:
                src, dst = pieces[i] if i < 4 else (wo_in, wo_mine)
                pltpu.make_async_copy(src, dst, swap_recv.at[group]).start()

    def wait_swap(group):
        wait(w.at[group, rows, :] if group < 3 else wo_mine, swap_recv.at[group])

    swap(0)

    hid_cp.wait()
    total = jnp.zeros((64, 256), F32)
    for i in range(32):
        v = hid[:, i * 256:(i + 1) * 256].astype(F32)
        total += v * v
    inv = lax.rsqrt(jnp.sum(total, axis=-1, keepdims=True) * (1.0 / 8192) + 1e-5)

    def slice_norm(r, store):
        yy = flip(yh, r[0]) * 2 + flip(yl, r[1])
        for zz in range(8):
            cols = at((zz * 4 + yy) * 256, 256)
            store(zz, (hid[:, cols].astype(F32) * inv * gain[:, cols]).astype(BF))

    def put0(zz, v):
        xs[0, k, x, :, zz * 256:(zz + 1) * 256] = v

    def put_norm(r):
        def put(zz, v):
            xn[r - 1, :, zz * 256:(zz + 1) * 256] = v
        slice_norm(RELS[r], put)

    slab_ref = xs.at[0, 0, 0]

    def to_sib(r, d):
        ref = xs.at[r, k, (x - d + 4) % 4]
        go("sib", ref, ref, sib, sib_recv.at[r] if r < 3 else last_sib_recv.at[d % 4])

    def wait_sib(r):
        wait(xs.at[r, 1 - k], sib_recv.at[r])

    def wait_last_sib(d):
        wait(slab_ref, last_sib_recv.at[d % 4])

    def spread(r):
        if r:
            wait(slab_ref, y_recv.at[r - 1])
        ref = xs.at[r, k, x]
        for i, d in enumerate((1, -1)):
            go("spread", ref, ref, xdev(d), xg_recv.at[r, i])
        to_sib(r, 0)

    def relay(r, d):
        wait(slab_ref, xg_recv.at[r, 0 if d == 1 else 1])
        ref = xs.at[r, k, (x - d + 4) % 4, pl.ds(0 if d == 1 else 32, 32)]
        go("relay", ref, ref, xdev(d), xh_recv.at[r])
        to_sib(r, d)

    def last(r):
        wait(slab_ref, xh_recv.at[r])
        to_sib(r, 2)

    def ring_ref(n, b, hf):
        if n < 3:
            return w.at[n, at(b * 256 + hf * 128, 128), :]
        return wo.at[b, at(k * 512 + hf * 256, 256), :]

    def ring_wait(n, i):
        wait(w.at[n, pl.ds(0, 256), :] if n < 3 else wo.at[0, pl.ds(0, 512), :], ring_recv.at[n, i])

    def share(b):
        ref = wo.at[b, at(k * 512, 512), :]
        go("share", ref, ref, sib, share_recv)

    def ring_half(n, s, hf):
        if s > 0:
            ring_wait(n, s * 2 - 2 + hf)
        for d in (1, -1):
            if s == 3 and hf != (0 if d == 1 else 1):
                continue
            ref = ring_ref(n, (z - d * s + 8) % 8, hf)
            go("ring%d" % n, ref, ref, zdev(d), ring_recv.at[n, min(s * 2 + hf, 6)])
        if n == 3 and hf == 1:
            share((z + s) % 8)
            if s:
                share((z - s + 8) % 8)

    def ring_end(n):
        ring_wait(n, 6)
        if n == 3:
            share((z + 4) % 8)

    near, pair = RELS[1], RELS[3]
    low, high = pl.ds(0, 32), pl.ds(32, 32)

    def send_sum(r, xx, half, cols):
        a, b = RELS[r]
        slot = 0 if a else 1
        go("sum%d" % slot, part.at[r, 1 - yl, xx, half, cols], got.at[slot, flip(yl, b), xx, half, cols],
           ydev(near if a else pair), got_recv.at[slot])

    def far_sem(i, b, g):
        return i * 6 + b * 3 + (0 if i and b else g)

    def comp(r, g):
        a, b = RELS[r]
        cols = pl.ds(g * 256, 256)

        def one(c, carry):
            o = jnp.dot(xs[r, c].reshape(256, 2048), w[g], preferred_element_type=F32)
            part[r, c, :, :, g * 256:(g + 1) * 256] = o.astype(BF).reshape(4, 64, 256)
            return carry
        lax.fori_loop(0, 2, one, 0)
        if a:
            go("far0", part.at[r, yl, :, low, cols], fa.at[1 - b, :, :, cols], ydev(pair), far_recv.at[far_sem(0, 1 - b, g)])
            go("far1", part.at[r, yl, :, high, cols], fb.at[1 - b, :, :, cols], ydev(near), far_recv.at[far_sem(1, 1 - b, g)])
            send_sum(r, slice(None), high, cols)
        else:
            send_sum(r, slice(None), low, cols)

    def comp_slab(r, d):
        xx = (x - d + 4) % 4
        lhs = xs[r, :, xx].reshape(128, 2048)

        def one(g, carry):
            o = jnp.dot(lhs, w[g], preferred_element_type=F32).astype(BF)
            part[r, :, xx, :, at(g * 256, 256)] = o.reshape(2, 64, 256)
            return carry
        lax.fori_loop(0, 3, one, 0)
        send_sum(r, xx, low, slice(None))

    folded = set()

    def fold(r, i):
        a, b = RELS[r]
        side, buf, half, rows32 = (0, fa, low, slice(0, 32)) if a else (1, fb, high, slice(32, 64))
        slabs = r == 3
        if not slabs:
            wait(buf.at[b, :, :, pl.ds(i * 256, 256)], far_recv.at[far_sem(side, b, i)])
        elif r not in folded:
            folded.add(r)
            wait(buf.at[b], far_recv.at[far_sem(side, b, 0)])
        if slabs:
            xx, cols = (x - i + 4) % 4, slice(0, 768)
            part[r, 1 - yl, xx, rows32, cols] = (
                part[r, 1 - yl, xx, rows32, cols].astype(F32) + buf[b, xx].astype(F32)).astype(BF)
            send_sum(r, xx, half, slice(None))
        else:
            cols = slice(i * 256, (i + 1) * 256)
            part[r, 1 - yl, :, rows32, cols] = (
                part[r, 1 - yl, :, rows32, cols].astype(F32) + buf[b, :, :, cols].astype(F32)).astype(BF)
            send_sum(r, slice(None), half, pl.ds(i * 256, 256))

    def send_slice(r):
        go("slice", xn.at[r - 1], xs.at[r, k, x], ydev(RELS[r]), y_recv.at[r - 1])

    tab = {}

    def tables():
        wait(segs.at[1], seg_sem)
        own_row = jnp.where(k == yl, segs[0, 0:1, :], segs[1, 0:1, :])
        i_col = lax.broadcasted_iota(jnp.int32, (512, 512), 0)
        i_row = lax.broadcasted_iota(jnp.int32, (512, 512), 1)
        seg_col = jnp.sum(jnp.where(i_col == i_row, own_row, 0.0), axis=1, keepdims=True)
        start = jnp.sum(jnp.where(own_row < seg_col, 1.0, 0.0), axis=1, keepdims=True)
        lane = lax.broadcasted_iota(jnp.int32, (1, HEAD), 1)
        freq = jnp.where(lane < 64, lane, lane - 64).astype(F32)
        inverse = jnp.exp(freq * (-2.0 * math.log(500000.0) / HEAD))
        pos = lax.broadcasted_iota(jnp.int32, (512, 1), 0).astype(F32) - start
        angles = pos * inverse
        cos = jnp.cos(angles)
        sin = jnp.where(lane < 64, -1.0, 1.0) * jnp.sin(angles)
        tab.update(start=start, cos=cos, sin=sin)

    put_norm(1)
    send_slice(1)
    slice_norm(RELS[0], put0)
    spread(0)
    swap(1)
    put_norm(2)
    put_norm(3)
    segs[0] = jnp.broadcast_to(seg[...].astype(F32), (8, 512))
    go("seg", segs.at[0], segs.at[1], sib, seg_sem)

    wait_swap(0)
    ring_half(0, 0, 0)
    ring_half(0, 0, 1)
    wait_swap(1)
    ring_half(1, 0, 0)
    ring_half(1, 0, 1)
    swap(2)
    ring_half(0, 1, 0)
    spread(1)
    send_slice(2)
    relay(0, -1)
    relay(0, 1)
    ring_half(0, 1, 1)
    wait_swap(2)
    ring_half(2, 0, 0)
    ring_half(2, 0, 1)
    swap(3)
    ring_half(1, 1, 0)
    ring_half(1, 1, 1)
    ring_half(0, 2, 0)
    ring_half(0, 2, 1)
    ring_half(2, 1, 0)
    relay(1, -1)
    relay(1, 1)
    spread(2)
    send_slice(3)
    ring_half(2, 1, 1)
    ring_half(1, 2, 0)
    last(0)
    tables()
    ring_half(1, 2, 1)
    ring_half(0, 3, 0)
    last(1)
    ring_half(0, 3, 1)
    ring_half(2, 2, 0)
    spread(3)
    ring_half(2, 2, 1)
    ring_half(1, 3, 0)
    relay(2, -1)
    relay(2, 1)
    ring_half(1, 3, 1)
    wait_sib(1)
    ring_end(0)
    comp(1, 0)
    wait_sib(0)
    comp(0, 0)
    ring_half(2, 3, 0)
    ring_half(2, 3, 1)
    wait_swap(3)
    ring_half(3, 0, 0)
    ring_half(3, 0, 1)
    relay(3, -1)
    relay(3, 1)
    ring_end(1)
    comp(1, 1)
    fold(0, 0)
    comp(0, 1)
    last(2)
    ring_end(2)
    comp(1, 2)
    comp(0, 2)
    wait_sib(2)
    comp(2, 0)
    last(3)
    fold(0, 1)
    fold(2, 0)
    ring_half(3, 1, 0)
    comp(2, 1)
    fold(2, 1)
    comp(2, 2)
    wait_last_sib(-1)
    comp_slab(3, -1)
    fold(0, 2)
    ring_half(3, 1, 1)
    wait_last_sib(0)
    comp_slab(3, 0)
    fold(2, 2)
    wait_last_sib(1)
    comp_slab(3, 1)
    wait_last_sib(2)
    comp_slab(3, 2)
    ring_half(3, 2, 0)
    fold(1, 0)
    ring_half(3, 2, 1)
    fold(1, 1)
    fold(1, 2)
    ring_half(3, 3, 0)
    fold(3, -1)
    fold(3, 0)
    fold(3, 1)
    fold(3, 2)
    ring_half(3, 3, 1)

    def rotate(u):
        return (u * cos_b + pltpu.roll(u, 64, axis=1) * sin_b).astype(BF)

    start, cos, sin = tab["start"], tab["cos"], tab["sin"]
    for slot in range(2):
        wait(got.at[slot], got_recv.at[slot])
    for b in (0, 1):
        r = SLOT[(0, b)]
        half = flip(yl, b)
        rows_b = at(half * 256, 256)
        cos_b = jnp.where(half == 0, cos[0:256], cos[256:512])
        sin_b = jnp.where(half == 0, sin[0:256], sin[256:512])
        for i in range(6):
            cols = slice(i * 128, (i + 1) * 128)
            u = part[r, yl, :, :, cols].astype(F32)
            for slot in range(2):
                u += got[slot, half, :, :, cols].astype(F32)
            u = u.reshape(256, 128)
            if i == 0:
                ks[rows_b, :] = rotate(u)
            elif i == 1:
                vs[rows_b, :] = u.astype(BF)
            else:
                qs[rows_b, (i - 2) * 128:(i - 1) * 128] = rotate(u)

    scale = 1.0 / math.sqrt(HEAD)

    def attend(i):
        lo, hi = i * 128, (i + 1) * 128
        q = jnp.concatenate([qs[lo:hi, j * 128:(j + 1) * 128] for j in range(4)], axis=0)
        s = lax.dot_general(q, ks[:hi], (((1,), (1,)), ((), ())), preferred_element_type=F32) * scale
        where_i = lax.broadcasted_iota(jnp.int32, (128, hi), 0) + lo
        where_s = lax.broadcasted_iota(jnp.int32, (128, hi), 1)
        ok = (where_s <= where_i) & (where_s >= start[lo:hi].astype(jnp.int32))
        s = jnp.where(ok[None], s.reshape(4, 128, hi), -1e30)
        e = jnp.exp(s - jnp.max(s, axis=-1, keepdims=True))
        weights = (e / jnp.sum(e, axis=-1, keepdims=True)).astype(BF)
        o = jnp.dot(weights.reshape(512, hi), vs[:hi], preferred_element_type=F32).astype(BF)
        for j in range(4):
            for half in (0, 1):
                mixed[i // 2, (i % 2) * 2 + half, :, j * 128:(j + 1) * 128] = (
                    o[j * 128 + half * 64:j * 128 + half * 64 + 64])

    order = ((2, 0, 0, 32), (2, 0, 32, 32), (2, 1, 0, 64), (1, 0, 0, 64), (3, 0, 0, 64),
             (1, 1, 0, 64), (3, 1, 0, 64), (0, 0, 0, 64), (0, 1, 0, 64))

    def mixed_refs(n, r):
        d, f, first, size = order[n]
        xx = (x + d) % 4
        l = flip(flip(yl, RELS[r][1]), f)
        ps = pl.ds(first, size)
        return mixed.at[l, xx, ps], m.at[yh, l, xx, ps, at(k * 512, 512)]

    def send_mixed(n):
        for r in (2, 1, 3):
            src, dst = mixed_refs(n, r)
            go("mixed%d" % r, src, dst, mdev(RELS[r]), m_recv.at[n])
        src, dst = mixed_refs(n, 0)

        @pl.when(k == yl)
        def _():
            pltpu.make_async_copy(src, dst, m_recv.at[n]).start()

        @pl.when(k != yl)
        def _():
            pltpu.make_async_remote_copy(
                src_ref=src, dst_ref=dst, send_sem=m_send, recv_sem=m_recv.at[n],
                device_id=sib, device_id_type=MESH).start()

    for i in range(4):
        attend(i)
    for n in range(len(order)):
        send_mixed(n)
    ring_end(3)
    wait(wo.at[:, pl.ds(0, 512), :], share_recv)

    lo_cols, hi_cols = pl.ds(0, 1024), pl.ds(1024, 1024)

    def comp_out(n):
        d, f, first, size = order[n]
        l = flip(yl, f)
        xx = (x + d) % 4
        ps = pl.ds(first, size)
        wait(m.at[:, l, xx, ps], m_recv.at[n])
        lhs = m[:, l, xx, first:first + size].reshape(2 * size, 1024)

        def some(lo, count):
            def one(i, carry):
                zz = lo + i
                o = jnp.dot(lhs, wo[zz], preferred_element_type=F32).astype(BF)
                part2[d, :, l, first:first + size, at(zz * 256, 256)] = o.reshape(2, size, 256)
                return carry
            lax.fori_loop(0, count, one, 0)
            if d == 2:
                i = 0 if lo >= 4 else 1
                go("fwd", part2.at[2, :, l, ps, pl.ds(lo * 256, count * 256)],
                   fwd.at[i, :, l, ps, pl.ds(lo % 4 * 256, count * 256)], xdev(1 if lo >= 4 else -1), fwd_recv.at[i, l])

        if n == 0:
            for lo in (4, 0, 6, 2):
                some(lo, 2)
        elif d == 2:
            some(4, 4)
            some(0, 4)
        else:
            some(0, 8)

    rel_order = (2, 1, 3, 0)

    def slab_at(r):
        return flip(yh, RELS[r][0]), flip(yl, RELS[r][1])

    def parts_of(r):
        return (slice(0, 32), slice(32, 64)) if r == 3 else (slice(0, 64),)

    def cross_sem(r, p):
        return cross_recv.at[r + p.start // 32]

    def send_side(r, d):
        a, l = slab_at(r)
        i, plain, cols = (0, lo_cols, slice(1024, 2048)) if d == 1 else (1, hi_cols, slice(0, 1024))
        pcols = pl.ds(cols.start, 1024)
        if r in (2, 1):
            wait(fwd.at[i, :, l], fwd_recv.at[i, l])
        for p in parts_of(r):
            ps = pl.ds(p.start, p.stop - p.start)
            go("cross", part2.at[d % 4, a, l, ps, plain], rx.at[i, r, ps, plain], xdev(d), cross_sem(r, p))
            part2[d % 4, a, l, p, cols] = (
                part2[d % 4, a, l, p, cols].astype(F32) + fwd[i, a, l, p].astype(F32)).astype(BF)
            go("cross", part2.at[d % 4, a, l, ps, pcols], rx.at[i, r, ps, pcols], xdev(d), cross_sem(r, p))

    for n in range(3):
        comp_out(n)
    for n, r, d in ((3, 2, 1), (4, 2, -1), (5, 1, 1), (6, 1, -1)):
        comp_out(n)
        send_side(r, d)
    for r in (3, 0):
        for d in (1, -1):
            send_side(r, d)
    for n in (7, 8):
        comp_out(n)

    for r in rel_order:
        a, l = slab_at(r)
        for p in parts_of(r):
            ps = pl.ds(p.start, p.stop - p.start)
            wait(rx.at[:, r, ps], cross_sem(r, p))
            o = (part2[0, a, l, p].astype(F32) + rx[0, r, p].astype(F32) + rx[1, r, p].astype(F32)).astype(BF)
            if r:
                slab[r - 1, p] = o
                go("last", slab.at[r - 1, ps], out.at[y_self, ps], ydev(RELS[r]), last_recv.at[r - 1])
            else:
                out[y_self] = o
    for r in (2, 1, 3):
        wait(slab.at[r - 1], last_recv.at[r - 1])

    @pl.when(k != yl)
    def _():
        wait(w.at[0, pl.ds(0, 1280), :], swap_send)
        wait(mixed, m_send)

    sent = dict(
        ring3=w.at[pl.ds(0, 2), pl.ds(0, 1792), :], spread=xs.at[0], relay=xs.at[0, 0], sib=xs.at[pl.ds(0, 2)], slice=xn,
        seg=segs.at[0], far0=fa, far1=fb, sum0=got.at[0], sum1=got.at[1], mixed1=mixed, mixed2=mixed, mixed3=mixed,
        share=wo.at[:, pl.ds(0, 512), :], fwd=fwd, cross=rx, last=slab)
    for n in range(3):
        sent["ring%d" % n] = w.at[n, pl.ds(0, 1792), :]
    for i, name in enumerate(SENDS):
        wait(sent[name], send.at[i])


V = pl.BlockSpec(memory_space=pltpu.VMEM)
ANY = pl.BlockSpec(memory_space=pl.ANY)
DMA = pltpu.SemaphoreType.DMA


def interleave_kernel(blocks, out):
    for y in range(4):
        for zz in range(8):
            out[:, (zz * 4 + y) * 256:(zz * 4 + y + 1) * 256] = blocks[y, :, zz * 256:(zz + 1) * 256]


def interleave(blocks):
    return pl.pallas_call(
        interleave_kernel,
        grid=(2,),
        out_shape=jax.ShapeDtypeStruct((64, 8192), BF),
        in_specs=[pl.BlockSpec((4, 32, 2048), lambda i: (0, i, 0))],
        out_specs=pl.BlockSpec((32, 8192), lambda i: (i, 0)),
        name="interleave",
    )(blocks)


def body(hidden, gain, segment_ids, w_query, key_matrix, value_matrix, w_out):
    blocks = pl.pallas_call(
        kernel,
        out_shape=jax.ShapeDtypeStruct((4, 64, 2048), BF),
        in_specs=[ANY, V, V, ANY, ANY, ANY, ANY],
        out_specs=V,
        scratch_shapes=[
            pltpu.VMEM((64, 8192), BF),
            pltpu.VMEM((3, 64, 2048), BF),
            pltpu.VMEM((4, 2, 4, 64, 2048), BF),
            pltpu.VMEM((3, 2048, 256), BF),
            pltpu.VMEM((8, 1024, 256), BF),
            pltpu.VMEM((4, 2, 4, 64, 768), BF),
            pltpu.VMEM((2, 2, 4, 64, 768), BF),
            pltpu.VMEM((2, 4, 32, 768), BF),
            pltpu.VMEM((2, 4, 32, 768), BF),
            pltpu.VMEM((2, 8, 512), F32),
            pltpu.VMEM((512, 512), BF),
            pltpu.VMEM((512, 128), BF),
            pltpu.VMEM((512, 128), BF),
            pltpu.VMEM((2, 4, 64, 512), BF),
            pltpu.VMEM((2, 2, 4, 64, 1024), BF),
            pltpu.VMEM((4, 2, 2, 64, 2048), BF),
            pltpu.VMEM((2, 2, 2, 64, 1024), BF),
            pltpu.VMEM((2, 4, 64, 2048), BF),
            pltpu.VMEM((3, 64, 2048), BF),
            DMA((len(SENDS),)), DMA, DMA, DMA, DMA((4,)),
            DMA((3,)), DMA((4, 2)), DMA((4,)), DMA((3,)), DMA((4,)),
            DMA((4, 7)), DMA((10,)), DMA, DMA((2,)),
            DMA, DMA((9,)), DMA((2, 2)), DMA((5,)), DMA((3,)),
        ],
        compiler_params=pltpu.CompilerParams(
            collective_id=0, has_side_effects=True, vmem_limit_bytes=VMEM_LIMIT),
        name="sublayer",
    )(hidden, gain.reshape(1, -1), segment_ids, w_query, key_matrix, value_matrix, w_out)
    return interleave(blocks)


def solution(mesh):
    placed = (
        P(("dp", "tensor"), None), P(), P("dp", None), P("dp", "tensor"),
        P("dp", "tensor"), P("dp", "tensor"), P("tensor", "dp"),
    )
    return jax.shard_map(
        body, mesh=mesh, in_specs=placed, out_specs=P(("dp", "tensor"), None), check_vma=False)
```

```python
import math

import jax
import jax.numpy as jnp
from jax import lax
from jax.experimental import pallas as pl
from jax.experimental.pallas import tpu as pltpu
from jax.sharding import PartitionSpec as P

MESH = pl.DeviceIdType.MESH
BF = jnp.bfloat16
F32 = jnp.float32
HEAD = 128
VMEM_LIMIT = 56 * 2**20

RELS = ((0, 0), (1, 1), (1, 0), (0, 1))
SLOT = {r: i for i, r in enumerate(RELS)}


def place():
    dp = lax.axis_index("dp")
    t = lax.axis_index("tensor")
    return t % 4, (dp // 2) % 2, t // 4, dp // 4, dp % 2


def device(x, yh, yl, z, k):
    return (z * 4 + yh * 2 + k, yl * 4 + x)


def flip(v, f):
    return 1 - v if f else v


def at(start, size):
    return pl.ds(pl.multiple_of(start, size), size)


SENDS = ("ring0", "ring1", "ring2", "ring3", "spread", "relay", "sib", "slice", "seg", "far0", "far1", "sum0", "sum1",
         "mixed1", "mixed2", "mixed3", "share", "fwd", "cross", "last")


def wait(ref, sem):
    pltpu.make_async_copy(ref, ref, sem).wait()


def kernel(hid_in, gain, seg, wq, wk, wv, wo_in, out,
           hid, xn, xs, w, wo, part, got, fa, fb, segs, qs, ks, vs, mixed, m, part2, fwd, rx, slab,
           send, hid_sem, seg_sem, swap_send, swap_recv, y_recv, xg_recv, xh_recv, sib_recv,
           ring_recv, far_recv, share_recv, got_recv, m_send, m_recv, fwd_recv, cross_recv, last_recv):
    x, yh, yl, z, k = place()
    y_self = yh * 2 + yl
    sib = device(x, yh, yl, z, 1 - k)
    swapped = device(x, yh, k, z, yl)

    def go(name, src, dst, dev, recv):
        pltpu.make_async_remote_copy(
            src_ref=src, dst_ref=dst, send_sem=send.at[SENDS.index(name)], recv_sem=recv,
            device_id=dev, device_id_type=MESH).start()

    def ydev(r):
        return device(x, flip(yh, r[0]), flip(yl, r[1]), z, k)

    def xdev(d):
        return device((x + d + 4) % 4, yh, yl, z, k)

    def zdev(d):
        return device(x, yh, yl, (z + d + 8) % 8, k)

    def mdev(r):
        return device(x, flip(yh, r[0]), flip(yl, r[1]), z, yl)

    hid_cp = pltpu.make_async_copy(hid_in, hid, hid_sem)
    hid_cp.start()

    bar = pltpu.get_barrier_semaphore()
    for dev in [ydev(r) for r in RELS[1:]] + [xdev(1), xdev(-1), zdev(1), zdev(-1), sib]:
        pl.semaphore_signal(bar, inc=1, device_id=dev, device_id_type=MESH)

    @pl.when(k != yl)
    def _():
        pl.semaphore_signal(bar, inc=1, device_id=swapped, device_id_type=MESH)

    for a in (0, 1):
        for j in (0, 1):
            src = device(x, flip(yh, a), k, z, j)
            if a == 0:
                @pl.when((k != yl) | (k != j))
                def _():
                    pl.semaphore_signal(bar, inc=1, device_id=src, device_id_type=MESH)
            else:
                pl.semaphore_signal(bar, inc=1, device_id=src, device_id_type=MESH)

    hid_cp.wait()
    total = jnp.zeros((64, 256), F32)
    for i in range(32):
        v = hid[:, i * 256:(i + 1) * 256].astype(F32)
        total += v * v
    inv = lax.rsqrt(jnp.sum(total, axis=-1, keepdims=True) * (1.0 / 8192) + 1e-5)

    def slice_norm(r, store):
        yy = flip(yh, r[0]) * 2 + flip(yl, r[1])
        for zz in range(8):
            cols = at((zz * 4 + yy) * 256, 256)
            store(zz, (hid[:, cols].astype(F32) * inv * gain[:, cols]).astype(BF))

    def put0(zz, v):
        xs[0, k, x, :, zz * 256:(zz + 1) * 256] = v

    def put_norm(r):
        def put(zz, v):
            xn[r - 1, :, zz * 256:(zz + 1) * 256] = v
        slice_norm(RELS[r], put)

    for r in (1, 2, 3):
        put_norm(r)
    slice_norm(RELS[0], put0)
    segs[0] = jnp.broadcast_to(seg[...].astype(F32), (8, 512))
    pl.semaphore_wait(bar, 11 + 2 * ((k + yl) % 2))

    rows = at(z * 256, 256)
    pieces = [
        (wk, w.at[0, rows, pl.ds(0, 128)]),
        (wv, w.at[0, rows, pl.ds(128, 128)]),
        (wq.at[:, pl.ds(0, 256)], w.at[1, rows, :]),
        (wq.at[:, pl.ds(256, 256)], w.at[2, rows, :]),
    ]
    wo_mine = wo.at[z, at(k * 512, 512), :]
    wo_theirs = wo.at[z, at(yl * 512, 512), :]

    groups = ((0, 1), (2,), (3,), (4,))

    def swap(group):
        @pl.when(k != yl)
        def _():
            for i in groups[group]:
                src, dst = pieces[i] if i < 4 else (wo_in, wo_theirs)
                pltpu.make_async_remote_copy(
                    src_ref=src, dst_ref=dst, send_sem=swap_send, recv_sem=swap_recv.at[group],
                    device_id=swapped, device_id_type=MESH).start()

        @pl.when(k == yl)
        def _():
            for i in groups[group]:
                src, dst = pieces[i] if i < 4 else (wo_in, wo_mine)
                pltpu.make_async_copy(src, dst, swap_recv.at[group]).start()

    def wait_swap(group):
        wait(w.at[group, rows, :] if group < 3 else wo_mine, swap_recv.at[group])

    slab_ref = xs.at[0, 0, 0]

    def to_sib(r, d):
        ref = xs.at[r, k, (x - d + 4) % 4]
        go("sib", ref, ref, sib, sib_recv.at[r])

    def wait_sib(r):
        wait(xs.at[r, 1 - k], sib_recv.at[r])

    def spread(r):
        if r:
            wait(slab_ref, y_recv.at[r - 1])
        ref = xs.at[r, k, x]
        for i, d in enumerate((1, -1)):
            go("spread", ref, ref, xdev(d), xg_recv.at[r, i])
        to_sib(r, 0)

    def relay(r, d):
        wait(slab_ref, xg_recv.at[r, 0 if d == 1 else 1])
        ref = xs.at[r, k, (x - d + 4) % 4, pl.ds(0 if d == 1 else 32, 32)]
        go("relay", ref, ref, xdev(d), xh_recv.at[r])
        to_sib(r, d)

    def last(r):
        wait(slab_ref, xh_recv.at[r])
        to_sib(r, 2)

    def ring_ref(n, b, hf):
        if n < 3:
            return w.at[n, at(b * 256 + hf * 128, 128), :]
        return wo.at[b, at(k * 512 + hf * 256, 256), :]

    def ring_wait(n, i):
        wait(w.at[n, pl.ds(0, 256), :] if n < 3 else wo.at[0, pl.ds(0, 512), :], ring_recv.at[n, i])

    def share(b):
        ref = wo.at[b, at(k * 512, 512), :]
        go("share", ref, ref, sib, share_recv)

    def ring_half(n, s, hf):
        if s > 0:
            ring_wait(n, s * 2 - 2 + hf)
        for d in (1, -1):
            if s == 3 and hf != (0 if d == 1 else 1):
                continue
            ref = ring_ref(n, (z - d * s + 8) % 8, hf)
            go("ring%d" % n, ref, ref, zdev(d), ring_recv.at[n, min(s * 2 + hf, 6)])
        if n == 3 and hf == 1:
            share((z + s) % 8)
            if s:
                share((z - s + 8) % 8)

    def ring_end(n):
        ring_wait(n, 6)
        if n == 3:
            share((z + 4) % 8)

    near, pair = RELS[1], RELS[3]
    low, high = pl.ds(0, 32), pl.ds(32, 32)

    def send_sum(r, xx, half, cols):
        a, b = RELS[r]
        slot = 0 if a else 1
        go("sum%d" % slot, part.at[r, 1 - yl, xx, half, cols], got.at[slot, flip(yl, b), xx, half, cols],
           ydev(near if a else pair), got_recv.at[slot])

    def far_sem(i, b, g):
        return i * 6 + b * 3 + g

    def comp(r, g):
        a, b = RELS[r]
        cols = pl.ds(g * 256, 256)

        def one(c, carry):
            o = jnp.dot(xs[r, c].reshape(256, 2048), w[g], preferred_element_type=F32)
            part[r, c, :, :, g * 256:(g + 1) * 256] = o.astype(BF).reshape(4, 64, 256)
            return carry
        lax.fori_loop(0, 2, one, 0)
        if a:
            go("far0", part.at[r, yl, :, low, cols], fa.at[1 - b, :, :, cols], ydev(pair), far_recv.at[far_sem(0, 1 - b, g)])
            go("far1", part.at[r, yl, :, high, cols], fb.at[1 - b, :, :, cols], ydev(near), far_recv.at[far_sem(1, 1 - b, g)])
            send_sum(r, slice(None), high, cols)
        else:
            send_sum(r, slice(None), low, cols)

    def fold(r, g):
        a, b = RELS[r]
        side, buf, half, rows32 = (0, fa, low, slice(0, 32)) if a else (1, fb, high, slice(32, 64))
        cols = slice(g * 256, (g + 1) * 256)
        wait(buf.at[b, :, :, pl.ds(g * 256, 256)], far_recv.at[far_sem(side, b, g)])
        part[r, 1 - yl, :, rows32, cols] = (
            part[r, 1 - yl, :, rows32, cols].astype(F32) + buf[b, :, :, cols].astype(F32)).astype(BF)
        send_sum(r, slice(None), half, pl.ds(g * 256, 256))

    def send_slice(r):
        go("slice", xn.at[r - 1], xs.at[r, k, x], ydev(RELS[r]), y_recv.at[r - 1])

    tab = {}

    def tables():
        wait(segs.at[1], seg_sem)
        own_row = jnp.where(k == yl, segs[0, 0:1, :], segs[1, 0:1, :])
        i_col = lax.broadcasted_iota(jnp.int32, (512, 512), 0)
        i_row = lax.broadcasted_iota(jnp.int32, (512, 512), 1)
        seg_col = jnp.sum(jnp.where(i_col == i_row, own_row, 0.0), axis=1, keepdims=True)
        start = jnp.sum(jnp.where(own_row < seg_col, 1.0, 0.0), axis=1, keepdims=True)
        lane = lax.broadcasted_iota(jnp.int32, (1, HEAD), 1)
        freq = jnp.where(lane < 64, lane, lane - 64).astype(F32)
        inverse = jnp.exp(freq * (-2.0 * math.log(500000.0) / HEAD))
        pos = lax.broadcasted_iota(jnp.int32, (512, 1), 0).astype(F32) - start
        angles = pos * inverse
        cos = jnp.cos(angles)
        sin = jnp.where(lane < 64, -1.0, 1.0) * jnp.sin(angles)
        tab.update(start=start, cos=cos, sin=sin)

    swap(0)
    send_slice(1)
    spread(0)
    swap(1)
    go("seg", segs.at[0], segs.at[1], sib, seg_sem)

    wait_swap(0)
    ring_half(0, 0, 0)
    ring_half(0, 0, 1)
    wait_swap(1)
    ring_half(1, 0, 0)
    ring_half(1, 0, 1)
    swap(2)
    ring_half(0, 1, 0)
    relay(0, -1)
    relay(0, 1)
    spread(1)
    send_slice(2)
    ring_half(0, 1, 1)
    wait_swap(2)
    ring_half(2, 0, 0)
    ring_half(2, 0, 1)
    swap(3)
    ring_half(1, 1, 0)
    ring_half(1, 1, 1)
    ring_half(0, 2, 0)
    last(0)
    tables()
    ring_half(0, 2, 1)
    ring_half(2, 1, 0)
    spread(2)
    send_slice(3)
    ring_half(2, 1, 1)
    ring_half(1, 2, 0)
    relay(1, -1)
    relay(1, 1)
    ring_half(1, 2, 1)
    ring_half(0, 3, 0)
    ring_half(0, 3, 1)
    ring_half(2, 2, 0)
    relay(2, -1)
    relay(2, 1)
    spread(3)
    ring_half(2, 2, 1)
    ring_half(1, 3, 0)
    last(1)
    ring_half(1, 3, 1)
    wait_sib(1)
    ring_end(0)
    comp(1, 0)
    ring_half(2, 3, 0)
    wait_swap(3)
    ring_half(3, 0, 0)
    wait_sib(0)
    comp(0, 0)
    ring_half(2, 3, 1)
    ring_half(3, 0, 1)
    last(2)
    ring_end(1)
    comp(1, 1)
    comp(0, 1)
    wait_sib(2)
    comp(2, 0)
    relay(3, -1)
    relay(3, 1)
    comp(2, 1)
    ring_half(3, 1, 0)
    ring_end(2)
    comp(1, 2)
    comp(2, 2)
    ring_half(3, 1, 1)
    comp(0, 2)
    last(3)
    fold(1, 0)
    fold(2, 0)
    fold(0, 0)
    ring_half(3, 2, 0)
    wait_sib(3)
    comp(3, 0)
    fold(3, 0)
    comp(3, 1)
    fold(1, 1)
    fold(2, 1)
    ring_half(3, 2, 1)
    comp(3, 2)
    fold(0, 1)
    fold(3, 1)
    ring_half(3, 3, 0)
    fold(1, 2)
    fold(2, 2)
    fold(0, 2)
    fold(3, 2)
    ring_half(3, 3, 1)
    ring_end(3)

    def rotate(u):
        return (u * cos_b + pltpu.roll(u, 64, axis=1) * sin_b).astype(BF)

    start, cos, sin = tab["start"], tab["cos"], tab["sin"]
    for slot in range(2):
        wait(got.at[slot], got_recv.at[slot])
    for b in (0, 1):
        r = SLOT[(0, b)]
        half = flip(yl, b)
        rows_b = at(half * 256, 256)
        cos_b = jnp.where(half == 0, cos[0:256], cos[256:512])
        sin_b = jnp.where(half == 0, sin[0:256], sin[256:512])
        for i in range(6):
            cols = slice(i * 128, (i + 1) * 128)
            u = part[r, yl, :, :, cols].astype(F32)
            for slot in range(2):
                u += got[slot, half, :, :, cols].astype(F32)
            u = u.reshape(256, 128)
            if i == 0:
                ks[rows_b, :] = rotate(u)
            elif i == 1:
                vs[rows_b, :] = u.astype(BF)
            else:
                qs[rows_b, (i - 2) * 128:(i - 1) * 128] = rotate(u)

    scale = 1.0 / math.sqrt(HEAD)

    def attend(i):
        lo, hi = i * 128, (i + 1) * 128
        q = jnp.concatenate([qs[lo:hi, j * 128:(j + 1) * 128] for j in range(4)], axis=0)
        s = lax.dot_general(q, ks[:hi], (((1,), (1,)), ((), ())), preferred_element_type=F32) * scale
        where_i = lax.broadcasted_iota(jnp.int32, (128, hi), 0) + lo
        where_s = lax.broadcasted_iota(jnp.int32, (128, hi), 1)
        ok = (where_s <= where_i) & (where_s >= start[lo:hi].astype(jnp.int32))
        s = jnp.where(ok[None], s.reshape(4, 128, hi), -1e30)
        e = jnp.exp(s - jnp.max(s, axis=-1, keepdims=True))
        weights = (e / jnp.sum(e, axis=-1, keepdims=True)).astype(BF)
        o = jnp.dot(weights.reshape(512, hi), vs[:hi], preferred_element_type=F32).astype(BF)
        for j in range(4):
            for half in (0, 1):
                mixed[i // 2, (i % 2) * 2 + half, :, j * 128:(j + 1) * 128] = (
                    o[j * 128 + half * 64:j * 128 + half * 64 + 64])

    order = ((2, 0, 0, 32), (2, 0, 32, 32), (2, 1, 0, 64), (1, 0, 0, 64), (3, 0, 0, 64),
             (1, 1, 0, 64), (3, 1, 0, 64), (0, 0, 0, 64), (0, 1, 0, 64))

    def mixed_refs(n, r):
        d, f, first, size = order[n]
        xx = (x + d) % 4
        l = flip(flip(yl, RELS[r][1]), f)
        ps = pl.ds(first, size)
        return mixed.at[l, xx, ps], m.at[yh, l, xx, ps, at(k * 512, 512)]

    def send_mixed(n):
        for r in (2, 1, 3):
            src, dst = mixed_refs(n, r)
            go("mixed%d" % r, src, dst, mdev(RELS[r]), m_recv.at[n])
        src, dst = mixed_refs(n, 0)

        @pl.when(k == yl)
        def _():
            pltpu.make_async_copy(src, dst, m_recv.at[n]).start()

        @pl.when(k != yl)
        def _():
            pltpu.make_async_remote_copy(
                src_ref=src, dst_ref=dst, send_sem=m_send, recv_sem=m_recv.at[n],
                device_id=sib, device_id_type=MESH).start()

    for i in range(4):
        attend(i)
    for n in range(len(order)):
        send_mixed(n)
    wait(wo.at[:, pl.ds(0, 512), :], share_recv)

    lo_cols, hi_cols = pl.ds(0, 1024), pl.ds(1024, 1024)

    def comp_out(n):
        d, f, first, size = order[n]
        l = flip(yl, f)
        xx = (x + d) % 4
        ps = pl.ds(first, size)
        wait(m.at[:, l, xx, ps], m_recv.at[n])
        lhs = m[:, l, xx, first:first + size].reshape(2 * size, 1024)

        def some(lo, count):
            def one(i, carry):
                zz = lo + i
                o = jnp.dot(lhs, wo[zz], preferred_element_type=F32).astype(BF)
                part2[d, :, l, first:first + size, at(zz * 256, 256)] = o.reshape(2, size, 256)
                return carry
            lax.fori_loop(0, count, one, 0)
            if d == 2:
                i = 0 if lo >= 4 else 1
                go("fwd", part2.at[2, :, l, ps, pl.ds(lo * 256, count * 256)],
                   fwd.at[i, :, l, ps, pl.ds(lo % 4 * 256, count * 256)], xdev(1 if lo >= 4 else -1), fwd_recv.at[i, l])

        if n == 0:
            for lo in (4, 0, 6, 2):
                some(lo, 2)
        elif d == 2:
            some(4, 4)
            some(0, 4)
        else:
            some(0, 8)

    rel_order = (2, 1, 3, 0)

    def slab_at(r):
        return flip(yh, RELS[r][0]), flip(yl, RELS[r][1])

    def parts_of(r):
        return (slice(0, 32), slice(32, 64)) if r == 3 else (slice(0, 64),)

    def cross_sem(r, p):
        return cross_recv.at[r + p.start // 32]

    def send_side(r, d):
        a, l = slab_at(r)
        i, plain, cols = (0, lo_cols, slice(1024, 2048)) if d == 1 else (1, hi_cols, slice(0, 1024))
        pcols = pl.ds(cols.start, 1024)
        if r in (2, 1):
            wait(fwd.at[i, :, l], fwd_recv.at[i, l])
        for p in parts_of(r):
            ps = pl.ds(p.start, p.stop - p.start)
            go("cross", part2.at[d % 4, a, l, ps, plain], rx.at[i, r, ps, plain], xdev(d), cross_sem(r, p))
            part2[d % 4, a, l, p, cols] = (
                part2[d % 4, a, l, p, cols].astype(F32) + fwd[i, a, l, p].astype(F32)).astype(BF)
            go("cross", part2.at[d % 4, a, l, ps, pcols], rx.at[i, r, ps, pcols], xdev(d), cross_sem(r, p))

    for n in range(3):
        comp_out(n)
    for n, r, d in ((3, 2, 1), (4, 2, -1), (5, 1, 1), (6, 1, -1)):
        comp_out(n)
        send_side(r, d)
    for r in (3, 0):
        for d in (1, -1):
            send_side(r, d)
    for n in (7, 8):
        comp_out(n)

    for r in rel_order:
        a, l = slab_at(r)
        for p in parts_of(r):
            ps = pl.ds(p.start, p.stop - p.start)
            wait(rx.at[:, r, ps], cross_sem(r, p))
            o = (part2[0, a, l, p].astype(F32) + rx[0, r, p].astype(F32) + rx[1, r, p].astype(F32)).astype(BF)
            if r:
                slab[r - 1, p] = o
                go("last", slab.at[r - 1, ps], out.at[y_self, ps], ydev(RELS[r]), last_recv.at[r - 1])
            else:
                slab[3] = o
                pltpu.make_async_copy(slab.at[3], out.at[y_self], last_recv.at[3]).start()
    for r in (2, 1, 3, 4):
        wait(slab.at[r - 1], last_recv.at[r - 1])

    @pl.when(k != yl)
    def _():
        wait(w.at[0, pl.ds(0, 1280), :], swap_send)
        wait(mixed, m_send)

    sent = dict(
        ring3=w.at[pl.ds(0, 2), pl.ds(0, 1792), :], spread=xs.at[0], relay=xs.at[0, 0], sib=xs.at[pl.ds(0, 2)], slice=xn,
        seg=segs.at[0], far0=fa, far1=fb, sum0=got.at[0], sum1=got.at[1], mixed1=mixed, mixed2=mixed, mixed3=mixed,
        share=wo.at[:, pl.ds(0, 512), :], fwd=fwd, cross=rx, last=slab.at[pl.ds(0, 3)])
    for n in range(3):
        sent["ring%d" % n] = w.at[n, pl.ds(0, 1792), :]
    for i, name in enumerate(SENDS):
        wait(sent[name], send.at[i])


V = pl.BlockSpec(memory_space=pltpu.VMEM)
ANY = pl.BlockSpec(memory_space=pl.ANY)
DMA = pltpu.SemaphoreType.DMA


def interleave_kernel(blocks, out):
    for y in range(4):
        for zz in range(8):
            out[:, (zz * 4 + y) * 256:(zz * 4 + y + 1) * 256] = blocks[y, :, zz * 256:(zz + 1) * 256]


def interleave(blocks):
    return pl.pallas_call(
        interleave_kernel,
        grid=(2,),
        out_shape=jax.ShapeDtypeStruct((64, 8192), BF),
        in_specs=[pl.BlockSpec((4, 32, 2048), lambda i: (0, i, 0))],
        out_specs=pl.BlockSpec((32, 8192), lambda i: (i, 0)),
        name="interleave",
    )(blocks)


def body(hidden, gain, segment_ids, w_query, key_matrix, value_matrix, w_out):
    blocks = pl.pallas_call(
        kernel,
        out_shape=jax.ShapeDtypeStruct((4, 64, 2048), BF),
        in_specs=[ANY, V, V, ANY, ANY, ANY, ANY],
        out_specs=ANY,
        scratch_shapes=[
            pltpu.VMEM((64, 8192), BF),
            pltpu.VMEM((3, 64, 2048), BF),
            pltpu.VMEM((4, 2, 4, 64, 2048), BF),
            pltpu.VMEM((3, 2048, 256), BF),
            pltpu.VMEM((8, 1024, 256), BF),
            pltpu.VMEM((4, 2, 4, 64, 768), BF),
            pltpu.VMEM((2, 2, 4, 64, 768), BF),
            pltpu.VMEM((2, 4, 32, 768), BF),
            pltpu.VMEM((2, 4, 32, 768), BF),
            pltpu.VMEM((2, 8, 512), F32),
            pltpu.VMEM((512, 512), BF),
            pltpu.VMEM((512, 128), BF),
            pltpu.VMEM((512, 128), BF),
            pltpu.VMEM((2, 4, 64, 512), BF),
            pltpu.VMEM((2, 2, 4, 64, 1024), BF),
            pltpu.VMEM((4, 2, 2, 64, 2048), BF),
            pltpu.VMEM((2, 2, 2, 64, 1024), BF),
            pltpu.VMEM((2, 4, 64, 2048), BF),
            pltpu.VMEM((4, 64, 2048), BF),
            DMA((len(SENDS),)), DMA, DMA, DMA, DMA((4,)),
            DMA((3,)), DMA((4, 2)), DMA((4,)), DMA((4,)),
            DMA((4, 7)), DMA((12,)), DMA, DMA((2,)),
            DMA, DMA((9,)), DMA((2, 2)), DMA((5,)), DMA((4,)),
        ],
        compiler_params=pltpu.CompilerParams(
            collective_id=0, has_side_effects=True, vmem_limit_bytes=VMEM_LIMIT),
        name="sublayer",
    )(hidden, gain.reshape(1, -1), segment_ids, w_query, key_matrix, value_matrix, w_out)
    return interleave(blocks)


def solution(mesh):
    placed = (
        P(("dp", "tensor"), None), P(), P("dp", None), P("dp", "tensor"),
        P("dp", "tensor"), P("dp", "tensor"), P("tensor", "dp"),
    )
    return jax.shard_map(
        body, mesh=mesh, in_specs=placed, out_specs=P(("dp", "tensor"), None), check_vma=False)
```

```python
import math

import jax
import jax.numpy as jnp
from jax import lax
from jax.experimental import pallas as pl
from jax.experimental.pallas import tpu as pltpu
from jax.sharding import PartitionSpec as P

MESH = pl.DeviceIdType.MESH
BF = jnp.bfloat16
F32 = jnp.float32
HEAD = 128
VMEM_LIMIT = 56 * 2**20

RELS = ((0, 0), (1, 1), (1, 0), (0, 1))
SLOT = {r: i for i, r in enumerate(RELS)}


def place():
    dp = lax.axis_index("dp")
    t = lax.axis_index("tensor")
    return t % 4, (dp // 2) % 2, t // 4, dp // 4, dp % 2


def device(x, yh, yl, z, k):
    return (z * 4 + yh * 2 + k, yl * 4 + x)


def flip(v, f):
    return 1 - v if f else v


def at(start, size):
    return pl.ds(pl.multiple_of(start, size), size)


SENDS = ("ring0", "ring1", "ring2", "ring3", "spread", "relay", "sib", "slice", "seg", "far0", "far1", "sum0", "sum1",
         "mixed1", "mixed2", "mixed3", "share", "fwd", "cross", "last")


def wait(ref, sem):
    pltpu.make_async_copy(ref, ref, sem).wait()


def kernel(hid_in, gain, seg, wq, wk, wv, wo_in, out,
           hid, xn, xs, w, wo, part, got, fa, fb, segs, qs, ks, vs, mixed, m, part2, fwd, rx, slab,
           send, hid_sem, seg_sem, swap_send, swap_recv, y_recv, xg_recv, xh_recv, sib_recv,
           ring_recv, far_recv, share_recv, got_recv, m_send, m_recv, fwd_recv, cross_recv, last_recv):
    x, yh, yl, z, k = place()
    y_self = yh * 2 + yl
    sib = device(x, yh, yl, z, 1 - k)
    swapped = device(x, yh, k, z, yl)

    def go(name, src, dst, dev, recv):
        pltpu.make_async_remote_copy(
            src_ref=src, dst_ref=dst, send_sem=send.at[SENDS.index(name)], recv_sem=recv,
            device_id=dev, device_id_type=MESH).start()

    def ydev(r):
        return device(x, flip(yh, r[0]), flip(yl, r[1]), z, k)

    def xdev(d):
        return device((x + d + 4) % 4, yh, yl, z, k)

    def zdev(d):
        return device(x, yh, yl, (z + d + 8) % 8, k)

    def mdev(r):
        return device(x, flip(yh, r[0]), flip(yl, r[1]), z, yl)

    hid_cp = pltpu.make_async_copy(hid_in, hid, hid_sem)
    hid_cp.start()

    bar = pltpu.get_barrier_semaphore()
    for dev in [ydev(r) for r in RELS[1:]] + [xdev(1), xdev(-1), zdev(1), zdev(-1), sib]:
        pl.semaphore_signal(bar, inc=1, device_id=dev, device_id_type=MESH)

    @pl.when(k != yl)
    def _():
        pl.semaphore_signal(bar, inc=1, device_id=swapped, device_id_type=MESH)

    for a in (0, 1):
        for j in (0, 1):
            src = device(x, flip(yh, a), k, z, j)
            if a == 0:
                @pl.when((k != yl) | (k != j))
                def _():
                    pl.semaphore_signal(bar, inc=1, device_id=src, device_id_type=MESH)
            else:
                pl.semaphore_signal(bar, inc=1, device_id=src, device_id_type=MESH)

    hid_cp.wait()
    total = jnp.zeros((64, 256), F32)
    for i in range(32):
        v = hid[:, i * 256:(i + 1) * 256].astype(F32)
        total += v * v
    inv = lax.rsqrt(jnp.sum(total, axis=-1, keepdims=True) * (1.0 / 8192) + 1e-5)

    def slice_norm(r, store):
        yy = flip(yh, r[0]) * 2 + flip(yl, r[1])
        for zz in range(8):
            cols = at((zz * 4 + yy) * 256, 256)
            store(zz, (hid[:, cols].astype(F32) * inv * gain[:, cols]).astype(BF))

    def put0(zz, v):
        xs[0, k, x, :, zz * 256:(zz + 1) * 256] = v

    def put_norm(r):
        def put(zz, v):
            xn[r - 1, :, zz * 256:(zz + 1) * 256] = v
        slice_norm(RELS[r], put)

    for r in (1, 2, 3):
        put_norm(r)
    slice_norm(RELS[0], put0)
    segs[0] = jnp.broadcast_to(seg[...].astype(F32), (8, 512))
    pl.semaphore_wait(bar, 11 + 2 * ((k + yl) % 2))

    rows = at(z * 256, 256)
    pieces = [
        (wk, w.at[0, rows, pl.ds(0, 128)]),
        (wv, w.at[0, rows, pl.ds(128, 128)]),
        (wq.at[:, pl.ds(0, 256)], w.at[1, rows, :]),
        (wq.at[:, pl.ds(256, 256)], w.at[2, rows, :]),
    ]
    wo_mine = wo.at[z, at(k * 512, 512), :]
    wo_theirs = wo.at[z, at(yl * 512, 512), :]

    groups = ((0, 1), (2,), (3,), (4,))

    def swap(group):
        @pl.when(k != yl)
        def _():
            for i in groups[group]:
                src, dst = pieces[i] if i < 4 else (wo_in, wo_theirs)
                pltpu.make_async_remote_copy(
                    src_ref=src, dst_ref=dst, send_sem=swap_send, recv_sem=swap_recv.at[group],
                    device_id=swapped, device_id_type=MESH).start()

        @pl.when(k == yl)
        def _():
            for i in groups[group]:
                src, dst = pieces[i] if i < 4 else (wo_in, wo_mine)
                pltpu.make_async_copy(src, dst, swap_recv.at[group]).start()

    def wait_swap(group):
        wait(w.at[group, rows, :] if group < 3 else wo_mine, swap_recv.at[group])

    slab_ref = xs.at[0, 0, 0]

    def to_sib(r, d):
        ref = xs.at[r, k, (x - d + 4) % 4]
        go("sib", ref, ref, sib, sib_recv.at[r])

    def wait_sib(r):
        wait(xs.at[r, 1 - k], sib_recv.at[r])

    def spread(r):
        if r:
            wait(slab_ref, y_recv.at[r - 1])
        ref = xs.at[r, k, x]
        for i, d in enumerate((1, -1)):
            go("spread", ref, ref, xdev(d), xg_recv.at[r, i])
        to_sib(r, 0)

    def relay(r, d):
        wait(slab_ref, xg_recv.at[r, 0 if d == 1 else 1])
        ref = xs.at[r, k, (x - d + 4) % 4, pl.ds(0 if d == 1 else 32, 32)]
        go("relay", ref, ref, xdev(d), xh_recv.at[r])
        to_sib(r, d)

    def last(r):
        wait(slab_ref, xh_recv.at[r])
        to_sib(r, 2)

    def ring_ref(n, b, hf):
        if n < 3:
            return w.at[n, at(b * 256 + hf * 128, 128), :]
        return wo.at[b, at(k * 512 + hf * 256, 256), :]

    def ring_wait(n, i):
        wait(w.at[n, pl.ds(0, 256), :] if n < 3 else wo.at[0, pl.ds(0, 512), :], ring_recv.at[n, i])

    def share(b):
        ref = wo.at[b, at(k * 512, 512), :]
        go("share", ref, ref, sib, share_recv)

    def ring_half(n, s, hf):
        if s > 0:
            ring_wait(n, s * 2 - 2 + hf)
        for d in (1, -1):
            if s == 3 and hf != (0 if d == 1 else 1):
                continue
            ref = ring_ref(n, (z - d * s + 8) % 8, hf)
            go("ring%d" % n, ref, ref, zdev(d), ring_recv.at[n, min(s * 2 + hf, 6)])
        if n == 3 and hf == 1:
            share((z + s) % 8)
            if s:
                share((z - s + 8) % 8)

    def ring_end(n):
        ring_wait(n, 6)
        if n == 3:
            share((z + 4) % 8)

    near, pair = RELS[1], RELS[3]
    low, high = pl.ds(0, 32), pl.ds(32, 32)

    def send_sum(r, xx, half, cols):
        a, b = RELS[r]
        slot = 0 if a else 1
        go("sum%d" % slot, part.at[r, 1 - yl, xx, half, cols], got.at[slot, flip(yl, b), xx, half, cols],
           ydev(near if a else pair), got_recv.at[slot])

    def far_sem(i, b, g):
        return i * 6 + b * 3 + g

    def comp(r, g):
        a, b = RELS[r]
        cols = pl.ds(g * 256, 256)

        def one(c, carry):
            o = jnp.dot(xs[r, c].reshape(256, 2048), w[g], preferred_element_type=F32)
            part[r, c, :, :, g * 256:(g + 1) * 256] = o.astype(BF).reshape(4, 64, 256)
            return carry
        lax.fori_loop(0, 2, one, 0)
        if a:
            go("far0", part.at[r, yl, :, low, cols], fa.at[1 - b, :, :, cols], ydev(pair), far_recv.at[far_sem(0, 1 - b, g)])
            go("far1", part.at[r, yl, :, high, cols], fb.at[1 - b, :, :, cols], ydev(near), far_recv.at[far_sem(1, 1 - b, g)])
            send_sum(r, slice(None), high, cols)
        else:
            send_sum(r, slice(None), low, cols)

    def fold(r, g):
        a, b = RELS[r]
        side, buf, half, rows32 = (0, fa, low, slice(0, 32)) if a else (1, fb, high, slice(32, 64))
        cols = slice(g * 256, (g + 1) * 256)
        wait(buf.at[b, :, :, pl.ds(g * 256, 256)], far_recv.at[far_sem(side, b, g)])
        part[r, 1 - yl, :, rows32, cols] = (
            part[r, 1 - yl, :, rows32, cols].astype(F32) + buf[b, :, :, cols].astype(F32)).astype(BF)
        send_sum(r, slice(None), half, pl.ds(g * 256, 256))

    def send_slice(r):
        go("slice", xn.at[r - 1], xs.at[r, k, x], ydev(RELS[r]), y_recv.at[r - 1])

    tab = {}

    def tables():
        wait(segs.at[1], seg_sem)
        own_row = jnp.where(k == yl, segs[0, 0:1, :], segs[1, 0:1, :])
        i_col = lax.broadcasted_iota(jnp.int32, (512, 512), 0)
        i_row = lax.broadcasted_iota(jnp.int32, (512, 512), 1)
        seg_col = jnp.sum(jnp.where(i_col == i_row, own_row, 0.0), axis=1, keepdims=True)
        start = jnp.sum(jnp.where(own_row < seg_col, 1.0, 0.0), axis=1, keepdims=True)
        lane = lax.broadcasted_iota(jnp.int32, (1, HEAD), 1)
        freq = jnp.where(lane < 64, lane, lane - 64).astype(F32)
        inverse = jnp.exp(freq * (-2.0 * math.log(500000.0) / HEAD))
        pos = lax.broadcasted_iota(jnp.int32, (512, 1), 0).astype(F32) - start
        angles = pos * inverse
        cos = jnp.cos(angles)
        sin = jnp.where(lane < 64, -1.0, 1.0) * jnp.sin(angles)
        tab.update(start=start, cos=cos, sin=sin)

    swap(0)
    send_slice(1)
    spread(0)
    swap(1)
    go("seg", segs.at[0], segs.at[1], sib, seg_sem)

    wait_swap(0)
    ring_half(0, 0, 0)
    ring_half(0, 0, 1)
    wait_swap(1)
    ring_half(1, 0, 0)
    ring_half(1, 0, 1)
    swap(2)
    ring_half(0, 1, 0)
    relay(0, -1)
    relay(0, 1)
    spread(1)
    send_slice(2)
    ring_half(0, 1, 1)
    wait_swap(2)
    ring_half(2, 0, 0)
    ring_half(2, 0, 1)
    swap(3)
    ring_half(1, 1, 0)
    ring_half(1, 1, 1)
    ring_half(0, 2, 0)
    last(0)
    tables()
    ring_half(0, 2, 1)
    ring_half(2, 1, 0)
    spread(2)
    send_slice(3)
    ring_half(2, 1, 1)
    ring_half(1, 2, 0)
    relay(1, -1)
    relay(1, 1)
    ring_half(1, 2, 1)
    ring_half(0, 3, 0)
    ring_half(0, 3, 1)
    ring_half(2, 2, 0)
    relay(2, -1)
    relay(2, 1)
    spread(3)
    ring_half(2, 2, 1)
    ring_half(1, 3, 0)
    last(1)
    ring_half(1, 3, 1)
    wait_sib(1)
    ring_end(0)
    comp(1, 0)
    ring_half(2, 3, 0)
    wait_swap(3)
    ring_half(3, 0, 0)
    wait_sib(0)
    comp(0, 0)
    ring_half(2, 3, 1)
    ring_half(3, 0, 1)
    last(2)
    ring_end(1)
    comp(1, 1)
    comp(0, 1)
    wait_sib(2)
    comp(2, 0)
    relay(3, -1)
    relay(3, 1)
    comp(2, 1)
    ring_half(3, 1, 0)
    ring_end(2)
    comp(1, 2)
    comp(2, 2)
    ring_half(3, 1, 1)
    comp(0, 2)
    last(3)
    fold(1, 0)
    fold(2, 0)
    fold(0, 0)
    ring_half(3, 2, 0)
    wait_sib(3)
    comp(3, 0)
    fold(3, 0)
    comp(3, 1)
    fold(1, 1)
    fold(2, 1)
    ring_half(3, 2, 1)
    comp(3, 2)
    fold(0, 1)
    fold(3, 1)
    ring_half(3, 3, 0)
    fold(1, 2)
    fold(2, 2)
    fold(0, 2)
    fold(3, 2)
    ring_half(3, 3, 1)
    ring_end(3)

    def rotate(u):
        return (u * cos_b + pltpu.roll(u, 64, axis=1) * sin_b).astype(BF)

    start, cos, sin = tab["start"], tab["cos"], tab["sin"]
    for slot in range(2):
        wait(got.at[slot], got_recv.at[slot])
    for b in (0, 1):
        r = SLOT[(0, b)]
        half = flip(yl, b)
        rows_b = at(half * 256, 256)
        cos_b = jnp.where(half == 0, cos[0:256], cos[256:512])
        sin_b = jnp.where(half == 0, sin[0:256], sin[256:512])
        for i in range(6):
            cols = slice(i * 128, (i + 1) * 128)
            u = part[r, yl, :, :, cols].astype(F32)
            for slot in range(2):
                u += got[slot, half, :, :, cols].astype(F32)
            u = u.reshape(256, 128)
            if i == 0:
                ks[rows_b, :] = rotate(u)
            elif i == 1:
                vs[rows_b, :] = u.astype(BF)
            else:
                qs[rows_b, (i - 2) * 128:(i - 1) * 128] = rotate(u)

    scale = 1.0 / math.sqrt(HEAD)

    def attend(i):
        lo, hi = i * 128, (i + 1) * 128
        q = jnp.concatenate([qs[lo:hi, j * 128:(j + 1) * 128] for j in range(4)], axis=0)
        s = lax.dot_general(q, ks[:hi], (((1,), (1,)), ((), ())), preferred_element_type=F32) * scale
        where_i = lax.broadcasted_iota(jnp.int32, (128, hi), 0) + lo
        where_s = lax.broadcasted_iota(jnp.int32, (128, hi), 1)
        ok = (where_s <= where_i) & (where_s >= start[lo:hi].astype(jnp.int32))
        s = jnp.where(ok[None], s.reshape(4, 128, hi), -1e30)
        e = jnp.exp(s - jnp.max(s, axis=-1, keepdims=True))
        weights = (e / jnp.sum(e, axis=-1, keepdims=True)).astype(BF)
        o = jnp.dot(weights.reshape(512, hi), vs[:hi], preferred_element_type=F32).astype(BF)
        for j in range(4):
            for half in (0, 1):
                mixed[i // 2, (i % 2) * 2 + half, :, j * 128:(j + 1) * 128] = (
                    o[j * 128 + half * 64:j * 128 + half * 64 + 64])

    order = ((2, 0, 0, 32), (2, 0, 32, 32), (2, 1, 0, 64), (1, 0, 0, 64), (3, 0, 0, 64),
             (1, 1, 0, 64), (3, 1, 0, 64), (0, 0, 0, 64), (0, 1, 0, 64))

    def mixed_refs(n, r):
        d, f, first, size = order[n]
        xx = (x + d) % 4
        l = flip(flip(yl, RELS[r][1]), f)
        ps = pl.ds(first, size)
        return mixed.at[l, xx, ps], m.at[yh, l, xx, ps, at(k * 512, 512)]

    def send_mixed(n):
        for r in (2, 1, 3):
            src, dst = mixed_refs(n, r)
            go("mixed%d" % r, src, dst, mdev(RELS[r]), m_recv.at[n])
        src, dst = mixed_refs(n, 0)

        @pl.when(k == yl)
        def _():
            pltpu.make_async_copy(src, dst, m_recv.at[n]).start()

        @pl.when(k != yl)
        def _():
            pltpu.make_async_remote_copy(
                src_ref=src, dst_ref=dst, send_sem=m_send, recv_sem=m_recv.at[n],
                device_id=sib, device_id_type=MESH).start()

    for i in range(4):
        attend(i)
    for n in range(len(order)):
        send_mixed(n)
    wait(wo.at[:, pl.ds(0, 512), :], share_recv)

    lo_cols, hi_cols = pl.ds(0, 1024), pl.ds(1024, 1024)

    def comp_out(n):
        d, f, first, size = order[n]
        l = flip(yl, f)
        xx = (x + d) % 4
        ps = pl.ds(first, size)
        wait(m.at[:, l, xx, ps], m_recv.at[n])
        lhs = m[:, l, xx, first:first + size].reshape(2 * size, 1024)

        def some(lo, count):
            def one(i, carry):
                zz = lo + i
                o = jnp.dot(lhs, wo[zz], preferred_element_type=F32).astype(BF)
                part2[d, :, l, first:first + size, at(zz * 256, 256)] = o.reshape(2, size, 256)
                return carry
            lax.fori_loop(0, count, one, 0)
            if d == 2:
                i = 0 if lo >= 4 else 1
                go("fwd", part2.at[2, :, l, ps, pl.ds(lo * 256, count * 256)],
                   fwd.at[i, :, l, ps, pl.ds(lo % 4 * 256, count * 256)], xdev(1 if lo >= 4 else -1), fwd_recv.at[i, l])

        if n == 0:
            for lo in (4, 0, 6, 2):
                some(lo, 2)
        elif d == 2:
            some(4, 4)
            some(0, 4)
        else:
            some(0, 8)

    rel_order = (2, 1, 3, 0)

    def slab_at(r):
        return flip(yh, RELS[r][0]), flip(yl, RELS[r][1])

    def parts_of(r):
        return (slice(0, 32), slice(32, 64)) if r in (3, 0) else (slice(0, 64),)

    def cross_sem(r, p):
        return cross_recv.at[r + p.start // 32 * (5 if r == 0 else 1)]

    def send_side(r, d):
        a, l = slab_at(r)
        i, plain, cols = (0, lo_cols, slice(1024, 2048)) if d == 1 else (1, hi_cols, slice(0, 1024))
        pcols = pl.ds(cols.start, 1024)
        if r in (2, 1):
            wait(fwd.at[i, :, l], fwd_recv.at[i, l])
        for p in parts_of(r):
            ps = pl.ds(p.start, p.stop - p.start)
            go("cross", part2.at[d % 4, a, l, ps, plain], rx.at[i, r, ps, plain], xdev(d), cross_sem(r, p))
            part2[d % 4, a, l, p, cols] = (
                part2[d % 4, a, l, p, cols].astype(F32) + fwd[i, a, l, p].astype(F32)).astype(BF)
            go("cross", part2.at[d % 4, a, l, ps, pcols], rx.at[i, r, ps, pcols], xdev(d), cross_sem(r, p))

    for n in range(3):
        comp_out(n)
    for n, r, d in ((3, 2, 1), (4, 2, -1), (5, 1, 1), (6, 1, -1)):
        comp_out(n)
        send_side(r, d)
    for r in (3, 0):
        for d in (1, -1):
            send_side(r, d)
    for n in (7, 8):
        comp_out(n)

    for r in rel_order:
        a, l = slab_at(r)
        for p in parts_of(r):
            ps = pl.ds(p.start, p.stop - p.start)
            wait(rx.at[:, r, ps], cross_sem(r, p))
            o = (part2[0, a, l, p].astype(F32) + rx[0, r, p].astype(F32) + rx[1, r, p].astype(F32)).astype(BF)
            if r:
                slab[r - 1, p] = o
                go("last", slab.at[r - 1, ps], out.at[y_self, ps], ydev(RELS[r]), last_recv.at[r - 1])
            else:
                slab[3, p] = o
                pltpu.make_async_copy(slab.at[3, ps], out.at[y_self, ps], last_recv.at[3]).start()
    for r in (2, 1, 3, 4):
        wait(slab.at[r - 1], last_recv.at[r - 1])

    @pl.when(k != yl)
    def _():
        wait(w.at[0, pl.ds(0, 1280), :], swap_send)
        wait(mixed, m_send)

    sent = dict(
        ring3=w.at[pl.ds(0, 2), pl.ds(0, 1792), :], spread=xs.at[0], relay=xs.at[0, 0], sib=xs.at[pl.ds(0, 2)], slice=xn,
        seg=segs.at[0], far0=fa, far1=fb, sum0=got.at[0], sum1=got.at[1], mixed1=mixed, mixed2=mixed, mixed3=mixed,
        share=wo.at[:, pl.ds(0, 512), :], fwd=fwd, cross=rx, last=slab.at[pl.ds(0, 3)])
    for n in range(3):
        sent["ring%d" % n] = w.at[n, pl.ds(0, 1792), :]
    for i, name in enumerate(SENDS):
        wait(sent[name], send.at[i])


V = pl.BlockSpec(memory_space=pltpu.VMEM)
ANY = pl.BlockSpec(memory_space=pl.ANY)
DMA = pltpu.SemaphoreType.DMA


def interleave_kernel(blocks, out):
    for y in range(4):
        for zz in range(8):
            out[:, (zz * 4 + y) * 256:(zz * 4 + y + 1) * 256] = blocks[y, :, zz * 256:(zz + 1) * 256]


def interleave(blocks):
    return pl.pallas_call(
        interleave_kernel,
        grid=(2,),
        out_shape=jax.ShapeDtypeStruct((64, 8192), BF),
        in_specs=[pl.BlockSpec((4, 32, 2048), lambda i: (0, i, 0))],
        out_specs=pl.BlockSpec((32, 8192), lambda i: (i, 0)),
        name="interleave",
    )(blocks)


def body(hidden, gain, segment_ids, w_query, key_matrix, value_matrix, w_out):
    blocks = pl.pallas_call(
        kernel,
        out_shape=jax.ShapeDtypeStruct((4, 64, 2048), BF),
        in_specs=[ANY, V, V, ANY, ANY, ANY, ANY],
        out_specs=ANY,
        scratch_shapes=[
            pltpu.VMEM((64, 8192), BF),
            pltpu.VMEM((3, 64, 2048), BF),
            pltpu.VMEM((4, 2, 4, 64, 2048), BF),
            pltpu.VMEM((3, 2048, 256), BF),
            pltpu.VMEM((8, 1024, 256), BF),
            pltpu.VMEM((4, 2, 4, 64, 768), BF),
            pltpu.VMEM((2, 2, 4, 64, 768), BF),
            pltpu.VMEM((2, 4, 32, 768), BF),
            pltpu.VMEM((2, 4, 32, 768), BF),
            pltpu.VMEM((2, 8, 512), F32),
            pltpu.VMEM((512, 512), BF),
            pltpu.VMEM((512, 128), BF),
            pltpu.VMEM((512, 128), BF),
            pltpu.VMEM((2, 4, 64, 512), BF),
            pltpu.VMEM((2, 2, 4, 64, 1024), BF),
            pltpu.VMEM((4, 2, 2, 64, 2048), BF),
            pltpu.VMEM((2, 2, 2, 64, 1024), BF),
            pltpu.VMEM((2, 4, 64, 2048), BF),
            pltpu.VMEM((4, 64, 2048), BF),
            DMA((len(SENDS),)), DMA, DMA, DMA, DMA((4,)),
            DMA((3,)), DMA((4, 2)), DMA((4,)), DMA((4,)),
            DMA((4, 7)), DMA((12,)), DMA, DMA((2,)),
            DMA, DMA((9,)), DMA((2, 2)), DMA((6,)), DMA((4,)),
        ],
        compiler_params=pltpu.CompilerParams(
            collective_id=0, has_side_effects=True, vmem_limit_bytes=VMEM_LIMIT),
        name="sublayer",
    )(hidden, gain.reshape(1, -1), segment_ids, w_query, key_matrix, value_matrix, w_out)
    return interleave(blocks)


def solution(mesh):
    placed = (
        P(("dp", "tensor"), None), P(), P("dp", None), P("dp", "tensor"),
        P("dp", "tensor"), P("dp", "tensor"), P("tensor", "dp"),
    )
    return jax.shard_map(
        body, mesh=mesh, in_specs=placed, out_specs=P(("dp", "tensor"), None), check_vma=False)
```

```python
import math

import jax
import jax.numpy as jnp
from jax import lax
from jax.experimental import pallas as pl
from jax.experimental.pallas import tpu as pltpu
from jax.sharding import PartitionSpec as P

MESH = pl.DeviceIdType.MESH
BF = jnp.bfloat16
F32 = jnp.float32
HEAD = 128
VMEM_LIMIT = 56 * 2**20

RELS = ((0, 0), (1, 1), (1, 0), (0, 1))
SLOT = {r: i for i, r in enumerate(RELS)}


def place():
    dp = lax.axis_index("dp")
    t = lax.axis_index("tensor")
    return t % 4, (dp // 2) % 2, t // 4, dp // 4, dp % 2


def device(x, yh, yl, z, k):
    return (z * 4 + yh * 2 + k, yl * 4 + x)


def flip(v, f):
    return 1 - v if f else v


def at(start, size):
    return pl.ds(pl.multiple_of(start, size), size)


SENDS = ("ring0", "ring1", "ring2", "ring3", "spread", "relay", "sib", "slice", "seg", "far0", "far1", "sum0", "sum1",
         "mixed1", "mixed2", "mixed3", "share", "fwd", "cross", "last")


def wait(ref, sem):
    pltpu.make_async_copy(ref, ref, sem).wait()


def kernel(hid_in, gain, seg, wq, wk, wv, wo_in, out,
           hid, xn, xs, w, wo, part, got, fa, fb, segs, qs, ks, vs, mixed, m, part2, fwd, rx, slab,
           send, hid_sem, seg_sem, swap_send, swap_recv, y_recv, xg_recv, xh_recv, sib_recv,
           ring_recv, far_recv, share_recv, got_recv, m_send, m_recv, fwd_recv, cross_recv, last_recv):
    x, yh, yl, z, k = place()
    y_self = yh * 2 + yl
    sib = device(x, yh, yl, z, 1 - k)
    swapped = device(x, yh, k, z, yl)

    def go(name, src, dst, dev, recv):
        pltpu.make_async_remote_copy(
            src_ref=src, dst_ref=dst, send_sem=send.at[SENDS.index(name)], recv_sem=recv,
            device_id=dev, device_id_type=MESH).start()

    def ydev(r):
        return device(x, flip(yh, r[0]), flip(yl, r[1]), z, k)

    def xdev(d):
        return device((x + d + 4) % 4, yh, yl, z, k)

    def zdev(d):
        return device(x, yh, yl, (z + d + 8) % 8, k)

    def mdev(r):
        return device(x, flip(yh, r[0]), flip(yl, r[1]), z, yl)

    hid_cp = pltpu.make_async_copy(hid_in, hid, hid_sem)
    hid_cp.start()

    bar = pltpu.get_barrier_semaphore()
    for dev in [ydev(r) for r in RELS[1:]] + [xdev(1), xdev(-1), zdev(1), zdev(-1), sib]:
        pl.semaphore_signal(bar, inc=1, device_id=dev, device_id_type=MESH)

    @pl.when(k != yl)
    def _():
        pl.semaphore_signal(bar, inc=1, device_id=swapped, device_id_type=MESH)

    for a in (0, 1):
        for j in (0, 1):
            src = device(x, flip(yh, a), k, z, j)
            if a == 0:
                @pl.when((k != yl) | (k != j))
                def _():
                    pl.semaphore_signal(bar, inc=1, device_id=src, device_id_type=MESH)
            else:
                pl.semaphore_signal(bar, inc=1, device_id=src, device_id_type=MESH)

    hid_cp.wait()
    total = jnp.zeros((64, 256), F32)
    for i in range(32):
        v = hid[:, i * 256:(i + 1) * 256].astype(F32)
        total += v * v
    inv = lax.rsqrt(jnp.sum(total, axis=-1, keepdims=True) * (1.0 / 8192) + 1e-5)

    def slice_norm(r, store):
        yy = flip(yh, r[0]) * 2 + flip(yl, r[1])
        for zz in range(8):
            cols = at((zz * 4 + yy) * 256, 256)
            store(zz, (hid[:, cols].astype(F32) * inv * gain[:, cols]).astype(BF))

    def put0(zz, v):
        xs[0, k, x, :, zz * 256:(zz + 1) * 256] = v

    def put_norm(r):
        def put(zz, v):
            xn[r - 1, :, zz * 256:(zz + 1) * 256] = v
        slice_norm(RELS[r], put)

    for r in (1, 2, 3):
        put_norm(r)
    slice_norm(RELS[0], put0)
    segs[0] = jnp.broadcast_to(seg[...].astype(F32), (8, 512))

    rows = at(z * 256, 256)
    pieces = [
        (wk, w.at[0, rows, pl.ds(0, 128)]),
        (wv, w.at[0, rows, pl.ds(128, 128)]),
        (wq.at[:, pl.ds(0, 256)], w.at[1, rows, :]),
        (wq.at[:, pl.ds(256, 256)], w.at[2, rows, :]),
    ]
    wo_mine = wo.at[z, at(k * 512, 512), :]
    wo_theirs = wo.at[z, at(yl * 512, 512), :]

    groups = ((0, 1), (2,), (3,), (4,))

    def swap(group):
        @pl.when(k != yl)
        def _():
            for i in groups[group]:
                src, dst = pieces[i] if i < 4 else (wo_in, wo_theirs)
                pltpu.make_async_remote_copy(
                    src_ref=src, dst_ref=dst, send_sem=swap_send, recv_sem=swap_recv.at[group],
                    device_id=swapped, device_id_type=MESH).start()

    def wait_swap(group):
        wait(w.at[group, rows, :] if group < 3 else wo_mine, swap_recv.at[group])

    slab_ref = xs.at[0, 0, 0]

    def to_sib(r, d):
        ref = xs.at[r, k, (x - d + 4) % 4]
        go("sib", ref, ref, sib, sib_recv.at[r])

    def wait_sib(r):
        wait(xs.at[r, 1 - k], sib_recv.at[r])

    def spread(r):
        if r:
            wait(slab_ref, y_recv.at[r - 1])
        ref = xs.at[r, k, x]
        for i, d in enumerate((1, -1)):
            go("spread", ref, ref, xdev(d), xg_recv.at[r, i])
        to_sib(r, 0)

    def relay(r, d):
        wait(slab_ref, xg_recv.at[r, 0 if d == 1 else 1])
        ref = xs.at[r, k, (x - d + 4) % 4, pl.ds(0 if d == 1 else 32, 32)]
        go("relay", ref, ref, xdev(d), xh_recv.at[r])
        to_sib(r, d)

    def last(r):
        wait(slab_ref, xh_recv.at[r])
        to_sib(r, 2)

    def ring_ref(n, b, hf):
        if n < 3:
            return w.at[n, at(b * 256 + hf * 128, 128), :]
        return wo.at[b, at(k * 512 + hf * 256, 256), :]

    def ring_wait(n, i):
        wait(w.at[n, pl.ds(0, 256), :] if n < 3 else wo.at[0, pl.ds(0, 512), :], ring_recv.at[n, i])

    def share(b):
        ref = wo.at[b, at(k * 512, 512), :]
        go("share", ref, ref, sib, share_recv)

    def ring_half(n, s, hf):
        if s > 0:
            ring_wait(n, s * 2 - 2 + hf)
        for d in (1, -1):
            if s == 3 and hf != (0 if d == 1 else 1):
                continue
            ref = ring_ref(n, (z - d * s + 8) % 8, hf)
            go("ring%d" % n, ref, ref, zdev(d), ring_recv.at[n, min(s * 2 + hf, 6)])
        if n == 3 and hf == 1:
            share((z + s) % 8)
            if s:
                share((z - s + 8) % 8)

    def ring_end(n):
        ring_wait(n, 6)
        if n == 3:
            share((z + 4) % 8)

    near, pair = RELS[1], RELS[3]
    low, high = pl.ds(0, 32), pl.ds(32, 32)

    def send_sum(r, xx, half, cols):
        a, b = RELS[r]
        slot = 0 if a else 1
        go("sum%d" % slot, part.at[r, 1 - yl, xx, half, cols], got.at[slot, flip(yl, b), xx, half, cols],
           ydev(near if a else pair), got_recv.at[slot])

    def far_sem(i, b, g):
        return i * 6 + b * 3 + g

    def comp(r, g):
        a, b = RELS[r]
        cols = pl.ds(g * 256, 256)

        def one(c, carry):
            o = jnp.dot(xs[r, c].reshape(256, 2048), w[g], preferred_element_type=F32)
            part[r, c, :, :, g * 256:(g + 1) * 256] = o.astype(BF).reshape(4, 64, 256)
            return carry
        lax.fori_loop(0, 2, one, 0)
        if a:
            go("far0", part.at[r, yl, :, low, cols], fa.at[1 - b, :, :, cols], ydev(pair), far_recv.at[far_sem(0, 1 - b, g)])
            go("far1", part.at[r, yl, :, high, cols], fb.at[1 - b, :, :, cols], ydev(near), far_recv.at[far_sem(1, 1 - b, g)])
            send_sum(r, slice(None), high, cols)
        else:
            send_sum(r, slice(None), low, cols)

    def fold(r, g):
        a, b = RELS[r]
        side, buf, half, rows32 = (0, fa, low, slice(0, 32)) if a else (1, fb, high, slice(32, 64))
        cols = slice(g * 256, (g + 1) * 256)
        wait(buf.at[b, :, :, pl.ds(g * 256, 256)], far_recv.at[far_sem(side, b, g)])
        part[r, 1 - yl, :, rows32, cols] = (
            part[r, 1 - yl, :, rows32, cols].astype(F32) + buf[b, :, :, cols].astype(F32)).astype(BF)
        send_sum(r, slice(None), half, pl.ds(g * 256, 256))

    def send_slice(r):
        go("slice", xn.at[r - 1], xs.at[r, k, x], ydev(RELS[r]), y_recv.at[r - 1])

    tab = {}

    def tables():
        wait(segs.at[1], seg_sem)
        own_row = jnp.where(k == yl, segs[0, 0:1, :], segs[1, 0:1, :])
        i_col = lax.broadcasted_iota(jnp.int32, (512, 512), 0)
        i_row = lax.broadcasted_iota(jnp.int32, (512, 512), 1)
        seg_col = jnp.sum(jnp.where(i_col == i_row, own_row, 0.0), axis=1, keepdims=True)
        start = jnp.sum(jnp.where(own_row < seg_col, 1.0, 0.0), axis=1, keepdims=True)
        lane = lax.broadcasted_iota(jnp.int32, (1, HEAD), 1)
        freq = jnp.where(lane < 64, lane, lane - 64).astype(F32)
        inverse = jnp.exp(freq * (-2.0 * math.log(500000.0) / HEAD))
        pos = lax.broadcasted_iota(jnp.int32, (512, 1), 0).astype(F32) - start
        angles = pos * inverse
        cos = jnp.cos(angles)
        sin = jnp.where(lane < 64, -1.0, 1.0) * jnp.sin(angles)
        tab.update(start=start, cos=cos, sin=sin)

    @pl.when(k == yl)
    def _():
        for group in range(4):
            for i in groups[group]:
                src, dst = pieces[i] if i < 4 else (wo_in, wo_mine)
                pltpu.make_async_copy(src, dst, swap_recv.at[group]).start()

    pl.semaphore_wait(bar, 11 + 2 * ((k + yl) % 2))
    swap(0)
    send_slice(1)
    spread(0)
    swap(1)
    go("seg", segs.at[0], segs.at[1], sib, seg_sem)

    wait_swap(0)
    ring_half(0, 0, 0)
    ring_half(0, 0, 1)
    wait_swap(1)
    ring_half(1, 0, 0)
    ring_half(1, 0, 1)
    swap(2)
    ring_half(0, 1, 0)
    relay(0, -1)
    relay(0, 1)
    spread(1)
    send_slice(2)
    ring_half(0, 1, 1)
    wait_swap(2)
    ring_half(2, 0, 0)
    ring_half(2, 0, 1)
    swap(3)
    ring_half(1, 1, 0)
    ring_half(1, 1, 1)
    ring_half(0, 2, 0)
    last(0)
    tables()
    ring_half(0, 2, 1)
    ring_half(2, 1, 0)
    spread(2)
    send_slice(3)
    ring_half(2, 1, 1)
    ring_half(1, 2, 0)
    relay(1, -1)
    relay(1, 1)
    ring_half(1, 2, 1)
    ring_half(0, 3, 0)
    ring_half(0, 3, 1)
    ring_half(2, 2, 0)
    relay(2, -1)
    relay(2, 1)
    spread(3)
    ring_half(2, 2, 1)
    ring_half(1, 3, 0)
    last(1)
    ring_half(1, 3, 1)
    wait_sib(1)
    ring_end(0)
    comp(1, 0)
    ring_half(2, 3, 0)
    wait_swap(3)
    ring_half(3, 0, 0)
    wait_sib(0)
    comp(0, 0)
    ring_half(2, 3, 1)
    ring_half(3, 0, 1)
    last(2)
    ring_end(1)
    comp(1, 1)
    comp(0, 1)
    wait_sib(2)
    comp(2, 0)
    relay(3, -1)
    relay(3, 1)
    comp(2, 1)
    ring_half(3, 1, 0)
    ring_end(2)
    comp(1, 2)
    comp(2, 2)
    ring_half(3, 1, 1)
    comp(0, 2)
    last(3)
    fold(1, 0)
    fold(2, 0)
    fold(0, 0)
    ring_half(3, 2, 0)
    wait_sib(3)
    comp(3, 0)
    fold(3, 0)
    comp(3, 1)
    fold(1, 1)
    fold(2, 1)
    ring_half(3, 2, 1)
    comp(3, 2)
    fold(0, 1)
    fold(3, 1)
    ring_half(3, 3, 0)
    fold(1, 2)
    fold(2, 2)
    fold(0, 2)
    fold(3, 2)
    ring_half(3, 3, 1)
    ring_end(3)

    def rotate(u):
        return (u * cos_b + pltpu.roll(u, 64, axis=1) * sin_b).astype(BF)

    start, cos, sin = tab["start"], tab["cos"], tab["sin"]
    for slot in range(2):
        wait(got.at[slot], got_recv.at[slot])
    for b in (0, 1):
        r = SLOT[(0, b)]
        half = flip(yl, b)
        rows_b = at(half * 256, 256)
        cos_b = jnp.where(half == 0, cos[0:256], cos[256:512])
        sin_b = jnp.where(half == 0, sin[0:256], sin[256:512])
        for i in range(6):
            cols = slice(i * 128, (i + 1) * 128)
            u = part[r, yl, :, :, cols].astype(F32)
            for slot in range(2):
                u += got[slot, half, :, :, cols].astype(F32)
            u = u.reshape(256, 128)
            if i == 0:
                ks[rows_b, :] = rotate(u)
            elif i == 1:
                vs[rows_b, :] = u.astype(BF)
            else:
                qs[rows_b, (i - 2) * 128:(i - 1) * 128] = rotate(u)

    scale = 1.0 / math.sqrt(HEAD)

    def attend(i):
        lo, hi = i * 128, (i + 1) * 128
        q = jnp.concatenate([qs[lo:hi, j * 128:(j + 1) * 128] for j in range(4)], axis=0)
        s = lax.dot_general(q, ks[:hi], (((1,), (1,)), ((), ())), preferred_element_type=F32) * scale
        where_i = lax.broadcasted_iota(jnp.int32, (128, hi), 0) + lo
        where_s = lax.broadcasted_iota(jnp.int32, (128, hi), 1)
        ok = (where_s <= where_i) & (where_s >= start[lo:hi].astype(jnp.int32))
        s = jnp.where(ok[None], s.reshape(4, 128, hi), -1e30)
        e = jnp.exp(s - jnp.max(s, axis=-1, keepdims=True))
        weights = (e / jnp.sum(e, axis=-1, keepdims=True)).astype(BF)
        o = jnp.dot(weights.reshape(512, hi), vs[:hi], preferred_element_type=F32).astype(BF)
        for j in range(4):
            for half in (0, 1):
                mixed[i // 2, (i % 2) * 2 + half, :, j * 128:(j + 1) * 128] = (
                    o[j * 128 + half * 64:j * 128 + half * 64 + 64])

    order = ((2, 0, 0, 32), (2, 0, 32, 32), (2, 1, 0, 64), (1, 0, 0, 64), (3, 0, 0, 64),
             (1, 1, 0, 64), (3, 1, 0, 64), (0, 0, 0, 64), (0, 1, 0, 64))

    def mixed_refs(n, r):
        d, f, first, size = order[n]
        xx = (x + d) % 4
        l = flip(flip(yl, RELS[r][1]), f)
        ps = pl.ds(first, size)
        return mixed.at[l, xx, ps], m.at[yh, l, xx, ps, at(k * 512, 512)]

    def send_mixed(n):
        for r in (2, 1, 3):
            src, dst = mixed_refs(n, r)
            go("mixed%d" % r, src, dst, mdev(RELS[r]), m_recv.at[n])
        src, dst = mixed_refs(n, 0)

        @pl.when(k == yl)
        def _():
            pltpu.make_async_copy(src, dst, m_recv.at[n]).start()

        @pl.when(k != yl)
        def _():
            pltpu.make_async_remote_copy(
                src_ref=src, dst_ref=dst, send_sem=m_send, recv_sem=m_recv.at[n],
                device_id=sib, device_id_type=MESH).start()

    for i in range(4):
        attend(i)
    for n in range(len(order)):
        send_mixed(n)
    wait(wo.at[:, pl.ds(0, 512), :], share_recv)

    lo_cols, hi_cols = pl.ds(0, 1024), pl.ds(1024, 1024)

    def comp_out(n):
        d, f, first, size = order[n]
        l = flip(yl, f)
        xx = (x + d) % 4
        ps = pl.ds(first, size)
        wait(m.at[:, l, xx, ps], m_recv.at[n])
        lhs = m[:, l, xx, first:first + size].reshape(2 * size, 1024)

        def some(lo, count):
            def one(i, carry):
                zz = lo + i
                o = jnp.dot(lhs, wo[zz], preferred_element_type=F32).astype(BF)
                part2[d, :, l, first:first + size, at(zz * 256, 256)] = o.reshape(2, size, 256)
                return carry
            lax.fori_loop(0, count, one, 0)
            if d == 2:
                i = 0 if lo >= 4 else 1
                go("fwd", part2.at[2, :, l, ps, pl.ds(lo * 256, count * 256)],
                   fwd.at[i, :, l, ps, pl.ds(lo % 4 * 256, count * 256)], xdev(1 if lo >= 4 else -1), fwd_recv.at[i, l])

        if n == 0:
            for lo in (4, 0, 6, 2):
                some(lo, 2)
        elif d == 2:
            some(4, 4)
            some(0, 4)
        else:
            some(0, 8)

    rel_order = (2, 1, 3, 0)

    def slab_at(r):
        return flip(yh, RELS[r][0]), flip(yl, RELS[r][1])

    def parts_of(r):
        return (slice(0, 32), slice(32, 64)) if r == 3 else (slice(0, 64),)

    def cross_sem(r, p):
        return cross_recv.at[r + p.start // 32]

    def send_side(r, d):
        a, l = slab_at(r)
        i, plain, cols = (0, lo_cols, slice(1024, 2048)) if d == 1 else (1, hi_cols, slice(0, 1024))
        pcols = pl.ds(cols.start, 1024)
        if r in (2, 1):
            wait(fwd.at[i, :, l], fwd_recv.at[i, l])
        for p in parts_of(r):
            ps = pl.ds(p.start, p.stop - p.start)
            go("cross", part2.at[d % 4, a, l, ps, plain], rx.at[i, r, ps, plain], xdev(d), cross_sem(r, p))
            part2[d % 4, a, l, p, cols] = (
                part2[d % 4, a, l, p, cols].astype(F32) + fwd[i, a, l, p].astype(F32)).astype(BF)
            go("cross", part2.at[d % 4, a, l, ps, pcols], rx.at[i, r, ps, pcols], xdev(d), cross_sem(r, p))

    for n in range(3):
        comp_out(n)
    for n, r, d in ((3, 2, 1), (4, 2, -1), (5, 1, 1), (6, 1, -1)):
        comp_out(n)
        send_side(r, d)
    for r in (3, 0):
        for d in (1, -1):
            send_side(r, d)
    for n in (7, 8):
        comp_out(n)

    for r in rel_order:
        a, l = slab_at(r)
        for p in parts_of(r):
            ps = pl.ds(p.start, p.stop - p.start)
            wait(rx.at[:, r, ps], cross_sem(r, p))
            o = (part2[0, a, l, p].astype(F32) + rx[0, r, p].astype(F32) + rx[1, r, p].astype(F32)).astype(BF)
            if r:
                slab[r - 1, p] = o
                go("last", slab.at[r - 1, ps], out.at[y_self, ps], ydev(RELS[r]), last_recv.at[r - 1])
            else:
                slab[3] = o
                pltpu.make_async_copy(slab.at[3], out.at[y_self], last_recv.at[3]).start()
    for r in (2, 1, 3, 4):
        wait(slab.at[r - 1], last_recv.at[r - 1])

    @pl.when(k != yl)
    def _():
        wait(w.at[0, pl.ds(0, 1280), :], swap_send)
        wait(mixed, m_send)

    sent = dict(
        ring3=w.at[pl.ds(0, 2), pl.ds(0, 1792), :], spread=xs.at[0], relay=xs.at[0, 0], sib=xs.at[pl.ds(0, 2)], slice=xn,
        seg=segs.at[0], far0=fa, far1=fb, sum0=got.at[0], sum1=got.at[1], mixed1=mixed, mixed2=mixed, mixed3=mixed,
        share=wo.at[:, pl.ds(0, 512), :], fwd=fwd, cross=rx, last=slab.at[pl.ds(0, 3)])
    for n in range(3):
        sent["ring%d" % n] = w.at[n, pl.ds(0, 1792), :]
    for i, name in enumerate(SENDS):
        wait(sent[name], send.at[i])


V = pl.BlockSpec(memory_space=pltpu.VMEM)
ANY = pl.BlockSpec(memory_space=pl.ANY)
DMA = pltpu.SemaphoreType.DMA


def interleave_kernel(blocks, out):
    for y in range(4):
        for zz in range(8):
            out[:, (zz * 4 + y) * 256:(zz * 4 + y + 1) * 256] = blocks[y, :, zz * 256:(zz + 1) * 256]


def interleave(blocks):
    return pl.pallas_call(
        interleave_kernel,
        grid=(2,),
        out_shape=jax.ShapeDtypeStruct((64, 8192), BF),
        in_specs=[pl.BlockSpec((4, 32, 2048), lambda i: (0, i, 0))],
        out_specs=pl.BlockSpec((32, 8192), lambda i: (i, 0)),
        name="interleave",
    )(blocks)


def body(hidden, gain, segment_ids, w_query, key_matrix, value_matrix, w_out):
    blocks = pl.pallas_call(
        kernel,
        out_shape=jax.ShapeDtypeStruct((4, 64, 2048), BF),
        in_specs=[ANY, V, V, ANY, ANY, ANY, ANY],
        out_specs=ANY,
        scratch_shapes=[
            pltpu.VMEM((64, 8192), BF),
            pltpu.VMEM((3, 64, 2048), BF),
            pltpu.VMEM((4, 2, 4, 64, 2048), BF),
            pltpu.VMEM((3, 2048, 256), BF),
            pltpu.VMEM((8, 1024, 256), BF),
            pltpu.VMEM((4, 2, 4, 64, 768), BF),
            pltpu.VMEM((2, 2, 4, 64, 768), BF),
            pltpu.VMEM((2, 4, 32, 768), BF),
            pltpu.VMEM((2, 4, 32, 768), BF),
            pltpu.VMEM((2, 8, 512), F32),
            pltpu.VMEM((512, 512), BF),
            pltpu.VMEM((512, 128), BF),
            pltpu.VMEM((512, 128), BF),
            pltpu.VMEM((2, 4, 64, 512), BF),
            pltpu.VMEM((2, 2, 4, 64, 1024), BF),
            pltpu.VMEM((4, 2, 2, 64, 2048), BF),
            pltpu.VMEM((2, 2, 2, 64, 1024), BF),
            pltpu.VMEM((2, 4, 64, 2048), BF),
            pltpu.VMEM((4, 64, 2048), BF),
            DMA((len(SENDS),)), DMA, DMA, DMA, DMA((4,)),
            DMA((3,)), DMA((4, 2)), DMA((4,)), DMA((4,)),
            DMA((4, 7)), DMA((12,)), DMA, DMA((2,)),
            DMA, DMA((9,)), DMA((2, 2)), DMA((5,)), DMA((4,)),
        ],
        compiler_params=pltpu.CompilerParams(
            collective_id=0, has_side_effects=True, vmem_limit_bytes=VMEM_LIMIT),
        name="sublayer",
    )(hidden, gain.reshape(1, -1), segment_ids, w_query, key_matrix, value_matrix, w_out)
    return interleave(blocks)


def solution(mesh):
    placed = (
        P(("dp", "tensor"), None), P(), P("dp", None), P("dp", "tensor"),
        P("dp", "tensor"), P("dp", "tensor"), P("tensor", "dp"),
    )
    return jax.shard_map(
        body, mesh=mesh, in_specs=placed, out_specs=P(("dp", "tensor"), None), check_vma=False)
```
